32 devices in a mesh: dp: 16 (over z, x, core), proto: 2 (over y).
Axes of the slice: x: 2, y: 2, z: 4, core: 2. Of those that a mesh axis runs over, the one named last changes fastest.
Arguments:
- packed: float32 [16384, 256], P('dp'), may hold values from -120 to 120
- crop_offsets: int32 [48], P('dp'), may hold values from 0 to 768, as said below
- masked_patch: int32 [3072], P('dp'), may hold values from 0 to 255, as said below
- teacher_logits: bfloat16 [3072, 65536], P('dp', 'proto'), may hold values from -6 to 26
- prototypes: float32 [65536, 256], P(('proto', 'dp')), may hold values from -4 to 4
- gain: float32 [65536], P(('proto', 'dp')), may hold values from 0.5 to 30
Outputs:
- grad_packed: float32 [16384, 256], P('dp')
- grad_proto: float32 [65536, 256], P(('proto', 'dp'))
- grad_gain: float32 [65536], P(('proto', 'dp'))
The draws below stay inside these ranges and needn't reach their ends.
Inputs may be any that keep to these rules, and one draw needn't show every extreme that they name: `crop_offsets`: within one index of dp the 3 crops of 256 rows lie inside the 1024 packed rows without intersecting, in increasing order. `masked_patch`: each crop has exactly 64 masked tokens, all with distinct patch indices; token t belongs to crop (t % 192) // 64 of its index of dp.
All inputs are finite; a program needn't handle non-finite values.
Results may differ from the reference program's by a relative error of at most 0.0003.
Values sent between devices are 32-bit elements; how exact they have to be, the bound alone decides.
No kernel may reach another device: no remote copies, remote signals or barrier semaphores. Data moves between devices by JAX's collectives and lax.ppermute only.
A program may use at most 256 MiB of HBM per device.

```python
import math
import jax
import jax.numpy as jnp
from jax import lax

E = 256
K = 65536
PACK_DEV = 1024
CROP_LEN = 256
CROPS = 3
MASK_CROP = 64
ITERS = 3
M_DEV = 192
TOKENS = 3072
N_DP = 16


def common_base(key):
    return jax.random.truncated_normal(jax.random.fold_in(key, 17), -6.0, 6.0, (K, E), jnp.float32)


def draw_prototypes(key, part):
    shared = common_base(key)
    key = jax.random.fold_in(key, 1)
    spread = jnp.exp(jax.random.uniform(key, (K, 1), jnp.float32, math.log(0.5), math.log(5.0)))
    return shared * spread / math.sqrt(E)


def draw_packed(key, part):
    key = jax.random.fold_in(key, 2)
    key_noise, key_scale = jax.random.split(key, 2)
    total_rows = PACK_DEV * N_DP
    noise = jax.random.truncated_normal(key_noise, -6.0, 6.0, (total_rows, E), jnp.float32)
    row_spread = jnp.exp(jax.random.uniform(key_scale, (total_rows, 1), jnp.float32, 0.0, math.log(10.0)))
    return row_spread * noise


def draw_gain(key, part):
    key = jax.random.fold_in(key, 3)
    lower, upper = (0.5, 4.0)
    return jnp.exp(jax.random.uniform(key, (K,), jnp.float32, math.log(lower), math.log(upper)))


def draw_teacher_logits(key, part):
    key = jax.random.fold_in(key, 4)
    key_vals = jax.random.fold_in(key, 0)
    return jax.random.truncated_normal(key_vals, -6.0, 6.0, (TOKENS, K), jnp.float32).astype(jnp.bfloat16)


def draw_crop_offsets(key, part):
    key = jax.random.fold_in(key, 5)
    spare = PACK_DEV - CROPS * CROP_LEN
    gaps = jnp.sort(jax.random.randint(key, (N_DP, CROPS), 0, spare + 1), axis=1)
    gaps = gaps.at[0, 0].set(0)
    gaps = gaps.at[N_DP - 1, CROPS - 1].set(spare)
    offsets = gaps + (jnp.arange(CROPS, dtype=jnp.int32) * CROP_LEN)[None, :]
    return offsets.reshape(N_DP * CROPS).astype(jnp.int32)


def draw_masked_patch(key, part):
    key = jax.random.fold_in(key, 6)
    crop_keys = jax.random.split(key, N_DP * CROPS)
    chosen = jax.vmap(lambda crop_key: jax.random.permutation(crop_key, CROP_LEN)[:MASK_CROP])(crop_keys)
    return chosen.reshape(TOKENS).astype(jnp.int32)


def setup_inputs(seed: int = 0) -> dict:
    seeds = jax.random.split(jax.random.key(seed), 7)
    return {
        "packed": draw_packed(jax.random.fold_in(seeds[6], 71), 0),
        "crop_offsets": draw_crop_offsets(jax.random.fold_in(seeds[6], 71), 0),
        "masked_patch": draw_masked_patch(jax.random.fold_in(seeds[6], 71), 0),
        "teacher_logits": draw_teacher_logits(jax.random.fold_in(seeds[6], 71), 0),
        "prototypes": draw_prototypes(jax.random.fold_in(seeds[6], 71), 0),
        "gain": draw_gain(jax.random.fold_in(seeds[6], 71), 0),
    }


HIGHEST = lax.Precision.HIGHEST
TEMP_S = 0.1
TEMP_T = 0.07
EPS = 1e-06

def reference(packed, crop_offsets, masked_patch, teacher_logits, prototypes, gain):
    tokens_all = jnp.arange(TOKENS, dtype=jnp.int32)
    dp_block = tokens_all // M_DEV
    crop_of = tokens_all % M_DEV // MASK_CROP
    row_index = (dp_block * PACK_DEV + crop_offsets[dp_block * CROPS + crop_of] + masked_patch).astype(jnp.int32)
    picked = packed[row_index]
    inverse = lax.rsqrt(lax.optimization_barrier(jnp.sum(picked * picked, axis=1, keepdims=True)) + EPS)
    unit_tok = picked * inverse
    proto_norm = jnp.sqrt(lax.optimization_barrier(jnp.sum(prototypes * prototypes, axis=1, keepdims=True)) + EPS)
    unit_proto = prototypes / proto_norm
    weights = unit_proto * (gain / TEMP_S)[:, None]
    height = math.gcd(TOKENS, 512)
    blocks = TOKENS // height
    block_ids = jnp.arange(blocks, dtype=jnp.int32)

    def base_block(block_index):
        scaled = lax.dynamic_slice_in_dim(teacher_logits, block_index * height, height, 0).astype(jnp.float32) / TEMP_T
        exponent = jnp.exp(scaled - lax.optimization_barrier(jnp.max(scaled, axis=1, keepdims=True)))
        return exponent / lax.optimization_barrier(jnp.sum(exponent, axis=1, keepdims=True))
    row_scale = jnp.ones((TOKENS,), jnp.float32)
    col_scale = jnp.ones((K,), jnp.float32)
    balance = TOKENS / K
    for sweep in range(ITERS):

        def column_body(running, block_index, row_scale=row_scale):
            part_rows = lax.dynamic_slice_in_dim(row_scale, block_index * height, height, 0)
            return (running + jnp.dot(part_rows, base_block(block_index), precision=HIGHEST), None)
        column_acc, _ = lax.scan(column_body, jnp.zeros((K,), jnp.float32), block_ids)
        column_sum = column_acc * col_scale
        col_scale = col_scale * balance / column_sum
        row_parts = lax.map(lambda block_index, col_scale=col_scale: jnp.dot(base_block(block_index), col_scale, precision=HIGHEST), block_ids)
        row_sum = row_parts.reshape(TOKENS) * row_scale
        row_scale = row_scale / row_sum
    loss_scale = K / math.sqrt(TOKENS)

    def final_body(running, block_index):
        tok_block = lax.dynamic_slice_in_dim(unit_tok, block_index * height, height, 0)
        logits = jnp.dot(tok_block, weights.T, precision=HIGHEST)
        student_max = lax.optimization_barrier(jnp.max(logits, axis=1, keepdims=True))
        exponent = jnp.exp(logits - student_max)
        student_prob = exponent / lax.optimization_barrier(jnp.sum(exponent, axis=1, keepdims=True))
        scale_rows = lax.dynamic_slice_in_dim(row_scale, block_index * height, height, 0)
        target = base_block(block_index) * scale_rows[:, None] * col_scale[None, :]
        grad_logits = loss_scale * (student_prob - target)
        running = running + lax.dot_general(grad_logits, tok_block, (((0,), (0,)), ((), ())), precision=HIGHEST)
        return (running, jnp.dot(grad_logits, weights, precision=HIGHEST))
    summed, token_parts = lax.scan(final_body, jnp.zeros((K, E), jnp.float32), block_ids)
    token_sum = token_parts.reshape(TOKENS, E)
    inner_dot = lax.optimization_barrier(jnp.sum(unit_tok * token_sum, axis=1, keepdims=True))
    input_grad = (token_sum - unit_tok * inner_dot) * inverse
    grad_packed = jnp.zeros((PACK_DEV * N_DP, E), jnp.float32).at[row_index].set(input_grad)
    gain_dot = lax.optimization_barrier(jnp.sum(unit_proto * summed, axis=1))
    grad_gain = gain_dot / TEMP_S
    grad_proto = gain[:, None] / (TEMP_S * proto_norm) * (summed - unit_proto * gain_dot[:, None])
    return (grad_packed, grad_proto, grad_gain)
```

```python
import math

import jax
import jax.numpy as jnp
import numpy as np
from jax import lax
from jax.experimental import pallas as pl
from jax.experimental.pallas import tpu as pltpu
from jax.sharding import PartitionSpec as P

ITERS = 3
TEMP_S = 0.1
TEMP_T = 0.07
EPS = 1e-06
LOG2E = math.log2(math.e)
TEACH = LOG2E / TEMP_T
LANES = 128
GROUP = 16
VMEM_LIMIT = 48 * 1024 * 1024
F32 = jnp.float32
BF16 = jnp.bfloat16


def params():
    return pltpu.CompilerParams(vmem_limit_bytes=VMEM_LIMIT)


def split(x):
    hi = x.astype(BF16)
    return hi, (x - hi.astype(F32)).astype(BF16)


def dot(a, b, dims=((1,), (0,))):
    return lax.dot_general(a, b, (dims, ((), ())), preferred_element_type=F32)


def teacher_kernel(t_ref, m_ref, s_ref, *, width, unroll):
    span = LANES * unroll
    for r in range(0, t_ref.shape[0], GROUP):

        def largest(step, best):
            base = pl.multiple_of(step * span, span)
            for j in range(unroll):
                x = t_ref[r : r + GROUP, pl.ds(base + j * LANES, LANES)].astype(F32)
                best = jnp.maximum(best, x)
            return best

        best = lax.fori_loop(0, width // span, largest, jnp.full((GROUP, LANES), -jnp.inf, F32))
        top = jnp.broadcast_to(jnp.max(best, axis=1, keepdims=True), (GROUP, LANES)) * TEACH

        def total(step, acc):
            base = pl.multiple_of(step * span, span)
            for j in range(unroll):
                x = t_ref[r : r + GROUP, pl.ds(base + j * LANES, LANES)].astype(F32)
                acc = acc + jnp.exp2(x * TEACH - top)
            return acc

        acc = lax.fori_loop(0, width // span, total, jnp.zeros((GROUP, LANES), F32))
        m_ref[r : r + GROUP, :] = top
        s_ref[r : r + GROUP, :] = acc


def teacher_stats(teacher):
    tokens, width = teacher.shape
    rows = 32
    shape = jax.ShapeDtypeStruct((tokens, LANES), F32)
    spec = pl.BlockSpec((rows, LANES), lambda i: (i, 0))
    return pl.pallas_call(
        lambda *refs: teacher_kernel(*refs, width=width, unroll=16),
        grid=(tokens // rows,),
        in_specs=[pl.BlockSpec((rows, width), lambda i: (i, 0))],
        out_specs=[spec, spec],
        out_shape=[shape, shape],
        compiler_params=params(),
        name="teacher_stats",
    )(teacher)


def column_kernel(t_ref, a_ref, r1_ref, r2_ref, out_ref, new_ref, *, unroll):
    tokens, block = t_ref.shape

    @pl.when(pl.program_id(0) == 0)
    def _():
        row = jnp.sum(r1_ref[...], axis=1, keepdims=True) + jnp.sum(r2_ref[...], axis=1, keepdims=True)
        new_ref[...] = a_ref[...] + jnp.broadcast_to(jnp.log(row) * LOG2E, new_ref.shape)

    span = LANES * unroll

    def chunk(step, carry):
        base = pl.multiple_of(step * span, span)
        accs = [jnp.zeros((8, LANES), F32) for _ in range(unroll)]
        for r in range(0, tokens, GROUP):
            offset = new_ref[r : r + GROUP, :]
            for j in range(unroll):
                x = t_ref[r : r + GROUP, pl.ds(base + j * LANES, LANES)].astype(F32)
                e = jnp.exp2(x * TEACH - offset)
                accs[j] = accs[j] + (e[:8] + e[8:])
        for j in range(unroll):
            out_ref[:, pl.ds(base + j * LANES, LANES)] = jnp.sum(accs[j], axis=0, keepdims=True)
        return carry

    lax.fori_loop(0, block // span, chunk, 0)


def column_pass(teacher, offset, row_here, row_there):
    tokens, width = teacher.shape
    block = min(width, 4096)
    whole = pl.BlockSpec((tokens, LANES), lambda i: (0, 0))
    return pl.pallas_call(
        lambda *refs: column_kernel(*refs, unroll=16),
        grid=(width // block,),
        in_specs=[pl.BlockSpec((tokens, block), lambda i: (0, i)), whole, whole, whole],
        out_specs=[pl.BlockSpec((1, block), lambda i: (0, i)), whole],
        out_shape=[
            jax.ShapeDtypeStruct((1, width), F32),
            jax.ShapeDtypeStruct((tokens, LANES), F32),
        ],
        compiler_params=params(),
        name="column_sums",
    )(teacher, offset, row_here, row_there)


def row_kernel(t_ref, a_ref, c1_ref, c2_ref, out_ref, col_ref, *, unroll, balance):
    tokens, block = t_ref.shape
    span = LANES * unroll
    col_ref[...] = balance / (c1_ref[...] + c2_ref[...])

    @pl.when(pl.program_id(0) == 0)
    def _():
        out_ref[...] = jnp.zeros_like(out_ref)

    def chunk(step, carry):
        base = pl.multiple_of(step * span, span)
        cols = [
            jnp.broadcast_to(col_ref[:, pl.ds(base + j * LANES, LANES)], (GROUP, LANES))
            for j in range(unroll)
        ]
        for r in range(0, tokens, GROUP):
            offset = a_ref[r : r + GROUP, :]
            acc = out_ref[r : r + GROUP, :]
            for j in range(unroll):
                x = t_ref[r : r + GROUP, pl.ds(base + j * LANES, LANES)].astype(F32)
                acc = acc + jnp.exp2(x * TEACH - offset) * cols[j]
            out_ref[r : r + GROUP, :] = acc
        return carry

    lax.fori_loop(0, block // span, chunk, 0)


def row_pass(teacher, offset, cols_here, cols_there, balance):
    tokens, width = teacher.shape
    block = min(width, 4096)
    whole = pl.BlockSpec((tokens, LANES), lambda i: (0, 0))
    cols = pl.BlockSpec((1, block), lambda i: (0, i))
    return pl.pallas_call(
        lambda *refs: row_kernel(*refs, unroll=16, balance=balance),
        grid=(width // block,),
        in_specs=[pl.BlockSpec((tokens, block), lambda i: (0, i)), whole, cols, cols],
        out_specs=[whole, cols],
        out_shape=[
            jax.ShapeDtypeStruct((tokens, LANES), F32),
            jax.ShapeDtypeStruct((1, width), F32),
        ],
        compiler_params=params(),
        name="row_sums",
    )(teacher, offset, cols_here, cols_there)


def student_kernel(u_ref, v_ref, w_ref, m_in, s_in, m_ref, s_ref):
    @pl.when(pl.program_id(0) == 0)
    def _():
        m_ref[...] = m_in[...]
        s_ref[...] = s_in[...]

    w_hi, w_lo = split(w_ref[...])
    last = ((1,), (1,))
    logits = dot(u_ref[...], w_hi, last) + (dot(u_ref[...], w_lo, last) + dot(v_ref[...], w_hi, last))
    tiles = [logits[:, j : j + LANES] for j in range(0, logits.shape[1], LANES)]
    best = m_ref[...]
    for tile in tiles:
        best = jnp.maximum(best, tile)
    total = s_ref[...] * jnp.exp2(m_ref[...] - best)
    for tile in tiles:
        total = total + jnp.exp2(tile - best)
    m_ref[...] = best
    s_ref[...] = total


def student_pass(u_hi, u_lo, weights, largest, total):
    tokens, depth = u_hi.shape
    rows = weights.shape[0]
    block = min(rows, 1024)
    tok = pl.BlockSpec((tokens, depth), lambda i: (0, 0))
    stat = pl.BlockSpec((tokens, LANES), lambda i: (0, 0))
    shape = jax.ShapeDtypeStruct((tokens, LANES), F32)
    return pl.pallas_call(
        student_kernel,
        grid=(rows // block,),
        in_specs=[tok, tok, pl.BlockSpec((block, depth), lambda i: (i, 0)), stat, stat],
        out_specs=[stat, stat],
        out_shape=[shape, shape],
        compiler_params=params(),
        name="student_stats",
    )(u_hi, u_lo, weights, largest, total)


def grad_kernel(*refs, streams):
    refs = list(refs)
    refs.pop(0)
    u_hi, u_lo, t_hi, t_lo, lse, offset, tok_in = refs[:7]
    teach = refs[7 : 7 + streams]
    cols = refs[7 + streams : 7 + 2 * streams]
    protos = refs[7 + 2 * streams : 7 + 3 * streams]
    outs = refs[7 + 3 * streams : 7 + 4 * streams]
    tok_out = refs[7 + 4 * streams]
    last = ((1,), (1,))
    token_part = tok_in[...]
    lse_col = lse[:, :1]
    off_col = offset[:, :1]
    for i in range(streams):
        w_hi, w_lo = split(protos[i][...])
        logits = dot(u_hi[...], w_hi, last) + (dot(u_hi[...], w_lo, last) + dot(u_lo[...], w_hi, last))
        student = jnp.exp2(logits - lse_col)
        target = jnp.exp2(teach[i][...].astype(F32) * TEACH - off_col) * cols[i][...]
        g_hi, g_lo = split(student - target)
        outs[i][...] = dot(t_hi[...], g_hi) + (dot(t_hi[...], g_lo) + dot(t_lo[...], g_hi))
        token_part = token_part + (dot(g_hi, w_hi) + (dot(g_hi, w_lo) + dot(g_lo, w_hi)))
    tok_out[...] = token_part


def grad_step(step, owners, tok, streams, consts, teacher, cols, weights):
    tokens, depth = tok.shape
    block = weights[0].shape[0] // (owners.shape[0] // 2)

    def way(i):
        return 0 if i < streams // 2 else 1

    def whole(shape):
        return pl.BlockSpec(shape, lambda g, own: (0, 0))

    def along(shape, i):
        return pl.BlockSpec(shape, lambda g, own: (0, own[2 * step + way(i)] * streams + i))

    def rows(shape, i):
        return pl.BlockSpec(shape, lambda g, own: (own[2 * step + way(i)], 0))

    each = range(streams)
    grid = pltpu.PrefetchScalarGridSpec(
        num_scalar_prefetch=1,
        grid=(1,),
        in_specs=[whole(c.shape) for c in consts]
        + [whole(tok.shape)]
        + [along((tokens, block), i) for i in each]
        + [along((1, block), i) for i in each]
        + [rows((block, depth), i) for i in each],
        out_specs=[whole((depth, block)) for i in each] + [whole(tok.shape)],
    )
    outs = pl.pallas_call(
        lambda *refs: grad_kernel(*refs, streams=streams),
        grid_spec=grid,
        out_shape=[jax.ShapeDtypeStruct((depth, block), F32) for i in each]
        + [jax.ShapeDtypeStruct(tok.shape, F32)],
        compiler_params=params(),
        name="grad_blocks",
    )(owners, *consts, tok, *([teacher] * streams), *([cols] * streams), *weights)
    return list(outs[:streams]), outs[streams]


def halves(count):
    return [1 << bit for bit in range(count.bit_length() - 1)]


def swap(x, axis, count, distance):
    return lax.ppermute(x, axis, [(i, i ^ distance) for i in range(count)])


def sum_pair(x, axis, count):
    steps = halves(count)
    for distance in steps[:-1]:
        x = x + swap(x, axis, count, distance)
    return x, swap(x, axis, count, steps[-1])


def log_total(largest, total, axis, count):
    stats = jnp.stack([largest, total])
    for distance in halves(count):
        other = swap(stats, axis, count, distance)
        top = jnp.maximum(stats[0], other[0])
        both = stats[1] * jnp.exp2(stats[0] - top) + other[1] * jnp.exp2(other[0] - top)
        stats = jnp.stack([top, both])
    return stats[0] + jnp.log2(stats[1])


def lane_stats(largest, total):
    top = jnp.max(largest, axis=1)
    return top, jnp.sum(total * jnp.exp2(largest - top[:, None]), axis=1)


def ring_order(count):
    depth = count // 4
    up = [z * 4 + core for z in range(depth) for core in range(2)]
    down = [z * 4 + 2 + core for z in reversed(range(depth)) for core in range(2)]
    return up + down


def body(packed, crop_offsets, masked_patch, teacher_logits, prototypes, gain):
    tokens_here = masked_patch.shape[0]
    crops_here = crop_offsets.shape[0]
    per_crop = tokens_here // crops_here
    dp_count = lax.axis_size("dp")
    proto_count = lax.axis_size("proto")
    slice_cols = teacher_logits.shape[1]
    shard = prototypes.shape[0]
    total_tokens = tokens_here * dp_count
    total_protos = slice_cols * proto_count
    loss_scale = total_protos / math.sqrt(total_tokens)
    balance = total_tokens / total_protos
    streams = 4 if shard % (4 * LANES) == 0 else 2
    block = shard // streams

    proto_norm = jnp.sqrt(jnp.sum(prototypes * prototypes, axis=1, keepdims=True) + EPS)
    unit_proto = prototypes / proto_norm
    weights = unit_proto * (gain / TEMP_S)[:, None]
    gathered = [
        lax.all_gather(weights[i * block : (i + 1) * block], "dp", axis=0, tiled=True)
        for i in range(streams)
    ]

    crop_of = jnp.arange(tokens_here, dtype=jnp.int32) // per_crop
    match = crop_of[:, None] == jnp.arange(crops_here, dtype=jnp.int32)[None, :]
    starts = jnp.sum(jnp.where(match, crop_offsets[None, :], 0), axis=1)
    row_index = starts + masked_patch
    picked = jnp.take(packed, row_index, axis=0)
    inverse = lax.rsqrt(jnp.sum(picked * picked, axis=1, keepdims=True) + EPS)
    unit_tok = picked * inverse

    def pieces(x):
        hi = lax.reduce_precision(x, 8, 7)
        return hi.astype(BF16), (x - hi).astype(BF16)

    u_hi, u_lo = pieces(unit_tok * LOG2E)
    t_hi, t_lo = pieces(unit_tok.T)

    top, total = teacher_stats(teacher_logits)
    base = log_total(top[:, 0], jnp.sum(total, axis=1), "proto", proto_count)
    offset = jnp.broadcast_to(base[:, None], (tokens_here, LANES))
    lane = lax.broadcasted_iota(jnp.int32, (tokens_here, LANES), 1)
    row_here = jnp.where(lane == 0, 1.0, 0.0).astype(F32)
    row_there = jnp.zeros((tokens_here, LANES), F32)
    for sweep in range(ITERS):
        sums, offset = column_pass(teacher_logits, offset, row_here, row_there)
        cols_here, cols_there = sum_pair(sums, "dp", dp_count)
        rows, cols = row_pass(teacher_logits, offset, cols_here, cols_there, balance)
        row_here, row_there = sum_pair(rows, "proto", proto_count)
    row_sum = jnp.sum(row_here, axis=1) + jnp.sum(row_there, axis=1)
    offset = offset + jnp.log2(row_sum)[:, None]
    cols = cols * loss_scale

    largest = jnp.full((tokens_here, LANES), -1e30, F32)
    total = jnp.zeros((tokens_here, LANES), F32)
    for piece in gathered:
        largest, total = student_pass(u_hi, u_lo, piece, largest, total)
    lse = log_total(*lane_stats(largest, total), "proto", proto_count) - math.log2(loss_scale)
    lse = jnp.broadcast_to(lse[:, None], (tokens_here, LANES))

    order = ring_order(dp_count)
    place = {d: p for p, d in enumerate(order)}
    table = np.zeros((dp_count, dp_count, 2), np.int32)
    for d in range(dp_count):
        for s in range(dp_count):
            table[d, s, 0] = order[(place[d] - 1 - s) % dp_count]
            table[d, s, 1] = order[(place[d] + 1 + s) % dp_count]
    owners = jnp.asarray(table.reshape(dp_count, -1))[lax.axis_index("dp")]
    ahead = [(d, order[(place[d] + 1) % dp_count]) for d in range(dp_count)]
    behind = [(d, order[(place[d] - 1) % dp_count]) for d in range(dp_count)]
    ways = [ahead if i < streams // 2 else behind for i in range(streams)]

    token_part = jnp.zeros(unit_tok.shape, F32)
    consts = (u_hi, u_lo, t_hi, t_lo, lse, offset)
    moving = None
    for step in range(dp_count):
        parts, token_part = grad_step(
            step, owners, token_part, streams, consts, teacher_logits, cols, gathered
        )
        if moving is not None:
            parts = [a + b for a, b in zip(parts, moving)]
        if step < dp_count - 1:
            moving = [lax.ppermute(x, "dp", way) for x, way in zip(parts, ways)]
    summed = jnp.concatenate([x.T for x in parts], axis=0)

    for distance in halves(proto_count):
        token_part = token_part + swap(token_part, "proto", proto_count, distance)
    inner_dot = jnp.sum(unit_tok * token_part, axis=1, keepdims=True)
    input_grad = (token_part - unit_tok * inner_dot) * inverse
    grad_packed = jnp.zeros(packed.shape, F32).at[row_index].set(input_grad)
    gain_dot = jnp.sum(unit_proto * summed, axis=1)
    grad_gain = gain_dot / TEMP_S
    grad_proto = gain[:, None] / (TEMP_S * proto_norm) * (summed - unit_proto * gain_dot[:, None])
    return (grad_packed, grad_proto, grad_gain)


def solution(mesh):
    placed = (
        P("dp", None),
        P("dp"),
        P("dp"),
        P("dp", "proto"),
        P(("proto", "dp"), None),
        P(("proto", "dp")),
    )
    return jax.shard_map(
        body,
        mesh=mesh,
        in_specs=placed,
        out_specs=(P("dp", None), P(("proto", "dp"), None), P(("proto", "dp"))),
        check_vma=False,
    )
```

```python
import math

import jax
import jax.numpy as jnp
import numpy as np
from jax import lax
from jax.experimental import pallas as pl
from jax.experimental.pallas import tpu as pltpu
from jax.sharding import PartitionSpec as P

ITERS = 3
TEMP_S = 0.1
TEMP_T = 0.07
EPS = 1e-06
LOG2E = math.log2(math.e)
TEACH = LOG2E / TEMP_T
LANES = 128
GROUP = 16
VMEM_LIMIT = 24 * 1024 * 1024
F32 = jnp.float32
BF16 = jnp.bfloat16


def params():
    return pltpu.CompilerParams(vmem_limit_bytes=VMEM_LIMIT)


def split(x):
    hi = x.astype(BF16)
    return hi, (x - hi.astype(F32)).astype(BF16)


def dot(a, b, dims=((1,), (0,))):
    return lax.dot_general(a, b, (dims, ((), ())), preferred_element_type=F32)


def teacher_kernel(t_ref, m_ref, s_ref, *, width, unroll):
    span = LANES * unroll
    for r in range(0, t_ref.shape[0], GROUP):

        def largest(step, best):
            base = pl.multiple_of(step * span, span)
            for j in range(unroll):
                x = t_ref[r : r + GROUP, pl.ds(base + j * LANES, LANES)].astype(F32)
                best = jnp.maximum(best, x)
            return best

        best = lax.fori_loop(0, width // span, largest, jnp.full((GROUP, LANES), -jnp.inf, F32))
        top = jnp.broadcast_to(jnp.max(best, axis=1, keepdims=True), (GROUP, LANES)) * TEACH

        def total(step, acc):
            base = pl.multiple_of(step * span, span)
            for j in range(unroll):
                x = t_ref[r : r + GROUP, pl.ds(base + j * LANES, LANES)].astype(F32)
                acc = acc + jnp.exp2(x * TEACH - top)
            return acc

        acc = lax.fori_loop(0, width // span, total, jnp.zeros((GROUP, LANES), F32))
        m_ref[r : r + GROUP, :] = top
        s_ref[r : r + GROUP, :] = acc


def teacher_stats(teacher):
    tokens, width = teacher.shape
    rows = 32
    shape = jax.ShapeDtypeStruct((tokens, LANES), F32)
    spec = pl.BlockSpec((rows, LANES), lambda i: (i, 0))
    return pl.pallas_call(
        lambda *refs: teacher_kernel(*refs, width=width, unroll=16),
        grid=(tokens // rows,),
        in_specs=[pl.BlockSpec((rows, width), lambda i: (i, 0))],
        out_specs=[spec, spec],
        out_shape=[shape, shape],
        compiler_params=params(),
        name="teacher_stats",
    )(teacher)


def column_kernel(t_ref, a_ref, r1_ref, r2_ref, out_ref, new_ref, *, unroll):
    tokens, block = t_ref.shape

    @pl.when(pl.program_id(0) == 0)
    def _():
        row = jnp.sum(r1_ref[...], axis=1, keepdims=True) + jnp.sum(r2_ref[...], axis=1, keepdims=True)
        new_ref[...] = a_ref[...] + jnp.broadcast_to(jnp.log(row) * LOG2E, new_ref.shape)

    span = LANES * unroll

    def chunk(step, carry):
        base = pl.multiple_of(step * span, span)
        accs = [jnp.zeros((8, LANES), F32) for _ in range(unroll)]
        for r in range(0, tokens, GROUP):
            offset = new_ref[r : r + GROUP, :]
            for j in range(unroll):
                x = t_ref[r : r + GROUP, pl.ds(base + j * LANES, LANES)].astype(F32)
                e = jnp.exp2(x * TEACH - offset)
                accs[j] = accs[j] + (e[:8] + e[8:])
        for j in range(unroll):
            out_ref[:, pl.ds(base + j * LANES, LANES)] = jnp.sum(accs[j], axis=0, keepdims=True)
        return carry

    lax.fori_loop(0, block // span, chunk, 0)


def column_pass(teacher, offset, row_here, row_there):
    tokens, width = teacher.shape
    block = min(width, 4096)
    whole = pl.BlockSpec((tokens, LANES), lambda i: (0, 0))
    return pl.pallas_call(
        lambda *refs: column_kernel(*refs, unroll=16),
        grid=(width // block,),
        in_specs=[pl.BlockSpec((tokens, block), lambda i: (0, i)), whole, whole, whole],
        out_specs=[pl.BlockSpec((1, block), lambda i: (0, i)), whole],
        out_shape=[
            jax.ShapeDtypeStruct((1, width), F32),
            jax.ShapeDtypeStruct((tokens, LANES), F32),
        ],
        compiler_params=params(),
        name="column_sums",
    )(teacher, offset, row_here, row_there)


def row_kernel(t_ref, a_ref, c1_ref, c2_ref, out_ref, col_ref, *, unroll, balance):
    tokens, block = t_ref.shape
    span = LANES * unroll
    col_ref[...] = balance / (c1_ref[...] + c2_ref[...])

    @pl.when(pl.program_id(0) == 0)
    def _():
        out_ref[...] = jnp.zeros_like(out_ref)

    def chunk(step, carry):
        base = pl.multiple_of(step * span, span)
        cols = [
            jnp.broadcast_to(col_ref[:, pl.ds(base + j * LANES, LANES)], (GROUP, LANES))
            for j in range(unroll)
        ]
        for r in range(0, tokens, GROUP):
            offset = a_ref[r : r + GROUP, :]
            acc = out_ref[r : r + GROUP, :]
            for j in range(unroll):
                x = t_ref[r : r + GROUP, pl.ds(base + j * LANES, LANES)].astype(F32)
                acc = acc + jnp.exp2(x * TEACH - offset) * cols[j]
            out_ref[r : r + GROUP, :] = acc
        return carry

    lax.fori_loop(0, block // span, chunk, 0)


def row_pass(teacher, offset, cols_here, cols_there, balance):
    tokens, width = teacher.shape
    block = min(width, 4096)
    whole = pl.BlockSpec((tokens, LANES), lambda i: (0, 0))
    cols = pl.BlockSpec((1, block), lambda i: (0, i))
    return pl.pallas_call(
        lambda *refs: row_kernel(*refs, unroll=16, balance=balance),
        grid=(width // block,),
        in_specs=[pl.BlockSpec((tokens, block), lambda i: (0, i)), whole, cols, cols],
        out_specs=[whole, cols],
        out_shape=[
            jax.ShapeDtypeStruct((tokens, LANES), F32),
            jax.ShapeDtypeStruct((1, width), F32),
        ],
        compiler_params=params(),
        name="row_sums",
    )(teacher, offset, cols_here, cols_there)


def parts_of_left(hi, lo, axis):
    return jnp.concatenate([hi, lo, hi], axis=axis)


def parts_of_right(hi, lo, axis):
    return jnp.concatenate([hi, hi, lo], axis=axis)


def student_kernel(u_ref, w_ref, m_ref, s_ref):
    tokens = u_ref.shape[1]

    @pl.when(pl.program_id(0) == 0)
    def _():
        m_ref[...] = jnp.full_like(m_ref, -1e30)
        s_ref[...] = jnp.zeros_like(s_ref)

    rows = w_ref.shape[0]
    chunk = min(rows, 512)
    for r in range(0, rows, chunk):
        w_hi, w_lo = split(w_ref[r : r + chunk, :])
        logits = dot(parts_of_left(w_hi, w_lo, 1), u_ref[...]).reshape(chunk // 8, 8, tokens)
        best = jnp.maximum(m_ref[...], jnp.max(logits, axis=0))
        fresh = jnp.sum(jnp.exp2(logits - best[None]), axis=0)
        s_ref[...] = s_ref[...] * jnp.exp2(m_ref[...] - best) + fresh
        m_ref[...] = best


def student_pass(u_turned, protos):
    tokens = u_turned.shape[1]
    rows, depth = protos.shape
    block = min(rows, 2048)
    stat = pl.BlockSpec((8, tokens), lambda i: (0, 0))
    shape = jax.ShapeDtypeStruct((8, tokens), F32)
    return pl.pallas_call(
        student_kernel,
        grid=(rows // block,),
        in_specs=[
            pl.BlockSpec(u_turned.shape, lambda i: (0, 0)),
            pl.BlockSpec((block, depth), lambda i: (i, 0)),
        ],
        out_specs=[stat, stat],
        out_shape=[shape, shape],
        compiler_params=params(),
        name="student_stats",
    )(u_turned, protos)


def grad_kernel(own, u_parts, t_parts, lse, offset, tok_in, *refs, moving):
    teach, cols, protos = refs[0:2], refs[2:4], refs[4:6]
    arrived = list(refs[6 : 6 + sum(moving)])
    outs = refs[6 + sum(moving) : 8 + sum(moving)]
    tok_out = refs[8 + sum(moving)]

    @pl.when(pl.program_id(0) == 0)
    def _():
        tok_out[...] = tok_in[...]

    token_part = tok_out[...]
    lse_col = lse[:, :1]
    off_col = offset[:, :1]
    for i in range(2):
        w_hi, w_lo = split(protos[i][...])
        logits = dot(u_parts[...], parts_of_right(w_hi, w_lo, 1), ((1,), (1,)))
        student = jnp.exp2(logits - lse_col)
        target = jnp.exp2(teach[i][...].astype(F32) * TEACH - off_col) * cols[i][...]
        g_hi, g_lo = split(student - target)
        part = dot(t_parts[...], parts_of_right(g_hi, g_lo, 0))
        if moving[i]:
            part = part + arrived.pop(0)[...]
        outs[i][...] = part
        token_part = token_part + dot(parts_of_left(g_hi, g_lo, 1), parts_of_right(w_hi, w_lo, 0))
    tok_out[...] = token_part


def grad_step(own, slots, consts, tok, teacher, cols, protos, arrived, width):
    tokens, depth = tok.shape
    block = min(width, 512)
    count = width // block

    def whole(shape):
        return pl.BlockSpec(shape, lambda g, own: (0, 0))

    def across(shape):
        return pl.BlockSpec(shape, lambda g, own: (0, g))

    def picked(shape, slot):
        return pl.BlockSpec(shape, lambda g, own: (0, own[slot] * count + g))

    def rows(shape, slot):
        return pl.BlockSpec(shape, lambda g, own: (own[slot] * count + g, 0))

    moving = tuple(x is not None for x in arrived)
    arrived = [x for x in arrived if x is not None]
    grid = pltpu.PrefetchScalarGridSpec(
        num_scalar_prefetch=1,
        grid=(count,),
        in_specs=[whole(c.shape) for c in consts]
        + [whole(tok.shape)]
        + [picked((tokens, block), slot) for slot in slots]
        + [picked((1, block), slot) for slot in slots]
        + [rows((block, depth), slot) for slot in slots]
        + [across((depth, block)) for x in arrived],
        out_specs=[across((depth, block)) for i in range(2)] + [whole(tok.shape)],
    )
    first, second, tok = pl.pallas_call(
        lambda *refs: grad_kernel(*refs, moving=moving),
        grid_spec=grid,
        out_shape=[jax.ShapeDtypeStruct((depth, width), F32) for i in range(2)]
        + [jax.ShapeDtypeStruct(tok.shape, F32)],
        compiler_params=params(),
        name="grad_blocks",
    )(own, *consts, tok, teacher, teacher, cols, cols, protos, protos, *arrived)
    return first, second, tok


def gather_kernel(*refs):
    for i in range(2):
        a, b, c = refs[3 * i : 3 * i + 3]
        refs[6][i] = (a[...] + (b[...] + c[...])).T


def own_sum(parts):
    depth, width = parts[0].shape
    block = min(width, 256)
    return pl.pallas_call(
        gather_kernel,
        grid=(width // block,),
        in_specs=[pl.BlockSpec((depth, block), lambda i: (0, i))] * 6,
        out_specs=pl.BlockSpec((2, block, depth), lambda i: (0, i, 0)),
        out_shape=jax.ShapeDtypeStruct((2, width, depth), F32),
        compiler_params=params(),
        name="own_sum",
    )(*parts).reshape(2 * width, depth)


def halves(count):
    return [1 << bit for bit in range(count.bit_length() - 1)]


def swap(x, axis, count, distance):
    return lax.ppermute(x, axis, [(i, i ^ distance) for i in range(count)])


def sum_pair(x, axis, count):
    steps = halves(count)
    for distance in steps[:-1]:
        x = x + swap(x, axis, count, distance)
    return x, swap(x, axis, count, steps[-1])


def log_total(largest, total, axis, count):
    stats = jnp.stack([largest, total])
    for distance in halves(count):
        other = swap(stats, axis, count, distance)
        top = jnp.maximum(stats[0], other[0])
        both = stats[1] * jnp.exp2(stats[0] - top) + other[1] * jnp.exp2(other[0] - top)
        stats = jnp.stack([top, both])
    return stats[0] + jnp.log2(stats[1])


def sublane_stats(largest, total):
    top = jnp.max(largest, axis=0)
    return top, jnp.sum(total * jnp.exp2(largest - top[None, :]), axis=0)


def ring_order(count):
    depth = count // 4
    up = [z * 4 + core for z in range(depth) for core in range(2)]
    down = [z * 4 + 2 + core for z in reversed(range(depth)) for core in range(2)]
    return up + down


def body(packed, crop_offsets, masked_patch, teacher_logits, prototypes, gain):
    tokens_here = masked_patch.shape[0]
    crops_here = crop_offsets.shape[0]
    per_crop = tokens_here // crops_here
    dp_count = lax.axis_size("dp")
    proto_count = lax.axis_size("proto")
    slice_cols = teacher_logits.shape[1]
    shard = prototypes.shape[0]
    total_tokens = tokens_here * dp_count
    total_protos = slice_cols * proto_count
    loss_scale = total_protos / math.sqrt(total_tokens)
    balance = total_tokens / total_protos
    width = shard // 2
    half = dp_count // 2

    order = ring_order(dp_count)
    place = {d: p for p, d in enumerate(order)}

    def around(step):
        return [(d, order[(place[d] + step) % dp_count]) for d in range(dp_count)]

    ahead, behind = around(1), around(-1)
    slot_of = np.zeros((dp_count, 2 * dp_count), np.int32)
    for d in range(dp_count):
        for far in range(dp_count):
            for sub in range(2):
                slot_of[d, 2 * far + sub] = 2 * order[(place[d] + far) % dp_count] + sub
    own = jnp.asarray(slot_of)[lax.axis_index("dp")]

    def slot(far, sub):
        return 2 * (far % dp_count) + sub

    proto_norm = jnp.sqrt(jnp.sum(prototypes * prototypes, axis=1, keepdims=True) + EPS)
    unit_proto = prototypes / proto_norm
    weights = unit_proto * (gain / TEMP_S)[:, None]
    gathered = lax.all_gather(weights, "dp", axis=0, tiled=True)

    crop_of = jnp.arange(tokens_here, dtype=jnp.int32) // per_crop
    match = crop_of[:, None] == jnp.arange(crops_here, dtype=jnp.int32)[None, :]
    starts = jnp.sum(jnp.where(match, crop_offsets[None, :], 0), axis=1)
    row_index = starts + masked_patch
    picked = jnp.take(packed, row_index, axis=0)
    inverse = lax.rsqrt(jnp.sum(picked * picked, axis=1, keepdims=True) + EPS)
    unit_tok = picked * inverse

    def pieces(x):
        hi = lax.reduce_precision(x, 8, 7)
        return hi.astype(BF16), (x - hi).astype(BF16)

    u_hi, u_lo = pieces(unit_tok * LOG2E)
    u_parts = parts_of_left(u_hi, u_lo, 1)
    u_turned = parts_of_right(u_hi, u_lo, 1).T
    t_parts = parts_of_left(*pieces(unit_tok.T), 1)

    top, total = teacher_stats(teacher_logits)
    base = log_total(top[:, 0], jnp.sum(total, axis=1), "proto", proto_count)
    offset = jnp.broadcast_to(base[:, None], (tokens_here, LANES))
    lane = lax.broadcasted_iota(jnp.int32, (tokens_here, LANES), 1)
    row_here = jnp.where(lane == 0, 1.0, 0.0).astype(F32)
    row_there = jnp.zeros((tokens_here, LANES), F32)
    for sweep in range(ITERS):
        sums, offset = column_pass(teacher_logits, offset, row_here, row_there)
        cols_here, cols_there = sum_pair(sums, "dp", dp_count)
        rows, cols = row_pass(teacher_logits, offset, cols_here, cols_there, balance)
        row_here, row_there = sum_pair(rows, "proto", proto_count)
    row_sum = jnp.sum(row_here, axis=1) + jnp.sum(row_there, axis=1)
    offset = offset + jnp.log2(row_sum)[:, None]
    cols = cols * loss_scale

    largest, total = student_pass(u_turned, gathered)
    lse = log_total(*sublane_stats(largest, total), "proto", proto_count) - math.log2(loss_scale)
    lse = jnp.broadcast_to(lse[:, None], (tokens_here, LANES))

    token_part = jnp.zeros(unit_tok.shape, F32)
    consts = (u_parts, t_parts, lse, offset)
    forward, backward, mine = [None, None], [None, None], [None, None]
    for step in range(half):
        for sub in range(2):
            up = half - step - sub
            down = half - 1 + sub - step
            one, two = slot(up, sub), slot(-down, sub)
            arrived = [forward[sub] if up else None, backward[sub] if down else None]
            first, second, token_part = grad_step(
                own,
                (one, two),
                consts,
                token_part,
                teacher_logits,
                cols,
                gathered,
                arrived,
                width,
            )
            if up:
                forward[sub] = lax.ppermute(first, "dp", ahead)
            else:
                mine[sub] = first
            if down:
                backward[sub] = lax.ppermute(second, "dp", behind)
            else:
                mine[sub] = second
    summed = own_sum([x for sub in range(2) for x in (mine[sub], forward[sub], backward[sub])])

    for distance in halves(proto_count):
        token_part = token_part + swap(token_part, "proto", proto_count, distance)
    inner_dot = jnp.sum(unit_tok * token_part, axis=1, keepdims=True)
    input_grad = (token_part - unit_tok * inner_dot) * inverse
    grad_packed = jnp.zeros(packed.shape, F32).at[row_index].set(input_grad)
    gain_dot = jnp.sum(unit_proto * summed, axis=1)
    grad_gain = gain_dot / TEMP_S
    grad_proto = gain[:, None] / (TEMP_S * proto_norm) * (summed - unit_proto * gain_dot[:, None])
    return (grad_packed, grad_proto, grad_gain)


def solution(mesh):
    placed = (
        P("dp", None),
        P("dp"),
        P("dp"),
        P("dp", "proto"),
        P(("proto", "dp"), None),
        P(("proto", "dp")),
    )
    return jax.shard_map(
        body,
        mesh=mesh,
        in_specs=placed,
        out_specs=(P("dp", None), P(("proto", "dp"), None), P(("proto", "dp"))),
        check_vma=False,
    )
```

```python
import math

import jax
import jax.numpy as jnp
import numpy as np
from jax import lax
from jax.experimental import pallas as pl
from jax.experimental.pallas import tpu as pltpu
from jax.sharding import PartitionSpec as P

ITERS = 3
TEMP_S = 0.1
TEMP_T = 0.07
EPS = 1e-06
LOG2E = math.log2(math.e)
TEACH = LOG2E / TEMP_T
LANES = 128
GROUP = 16
VMEM_LIMIT = 20 * 1024 * 1024
F32 = jnp.float32
BF16 = jnp.bfloat16


def params():
    return pltpu.CompilerParams(vmem_limit_bytes=VMEM_LIMIT)


def split(x):
    hi = x.astype(BF16)
    return hi, (x - hi.astype(F32)).astype(BF16)


def dot(a, b, dims=((1,), (0,))):
    return lax.dot_general(a, b, (dims, ((), ())), preferred_element_type=F32)


def teacher_kernel(t_ref, m_ref, s_ref, copy_ref, *, width, unroll):
    copy_ref[...] = t_ref[...]
    span = LANES * unroll
    for r in range(0, t_ref.shape[0], GROUP):

        def largest(step, best):
            base = pl.multiple_of(step * span, span)
            for j in range(unroll):
                x = t_ref[r : r + GROUP, pl.ds(base + j * LANES, LANES)].astype(F32)
                best = jnp.maximum(best, x)
            return best

        best = lax.fori_loop(0, width // span, largest, jnp.full((GROUP, LANES), -jnp.inf, F32))
        top = jnp.broadcast_to(jnp.max(best, axis=1, keepdims=True), (GROUP, LANES)) * TEACH

        def total(step, acc):
            base = pl.multiple_of(step * span, span)
            for j in range(unroll):
                x = t_ref[r : r + GROUP, pl.ds(base + j * LANES, LANES)].astype(F32)
                acc = acc + jnp.exp2(x * TEACH - top)
            return acc

        acc = lax.fori_loop(0, width // span, total, jnp.zeros((GROUP, LANES), F32))
        m_ref[r : r + GROUP, :] = top
        s_ref[r : r + GROUP, :] = acc


def teacher_stats(teacher):
    tokens, width = teacher.shape
    rows = 32
    shape = jax.ShapeDtypeStruct((tokens, LANES), F32)
    spec = pl.BlockSpec((rows, LANES), lambda i: (i, 0))
    return pl.pallas_call(
        lambda *refs: teacher_kernel(*refs, width=width, unroll=16),
        grid=(tokens // rows,),
        in_specs=[pl.BlockSpec((rows, width), lambda i: (i, 0))],
        out_specs=[spec, spec, pl.BlockSpec((rows, width), lambda i: (i, 0))],
        out_shape=[shape, shape, jax.ShapeDtypeStruct(teacher.shape, teacher.dtype)],
        compiler_params=params(),
        name="teacher_stats",
    )(teacher)


def column_kernel(t_ref, a_ref, r1_ref, r2_ref, out_ref, new_ref, *, unroll):
    tokens, block = t_ref.shape

    @pl.when(pl.program_id(0) == 0)
    def _():
        total = jnp.sum(r1_ref[...], axis=1, keepdims=True) + jnp.sum(r2_ref[...], axis=1, keepdims=True)
        new_ref[...] = a_ref[...] + jnp.broadcast_to(jnp.log(total) * LOG2E, new_ref.shape)

    span = LANES * unroll

    def chunk(step, carry):
        base = pl.multiple_of(step * span, span)
        accs = [jnp.zeros((8, LANES), F32) for _ in range(unroll)]
        for r in range(0, tokens, GROUP):
            offset = new_ref[r : r + GROUP, :]
            for j in range(unroll):
                x = t_ref[r : r + GROUP, pl.ds(base + j * LANES, LANES)].astype(F32)
                e = jnp.exp2(x * TEACH - offset)
                accs[j] = accs[j] + (e[:8] + e[8:])
        for j in range(unroll):
            out_ref[0, :, pl.ds(base + j * LANES, LANES)] = jnp.sum(
                accs[j], axis=0, keepdims=True
            )
        return carry

    lax.fori_loop(0, block // span, chunk, 0)


def column_pass(teacher, offset, row_here, row_there, shard):
    tokens, width = teacher.shape
    block = shard
    owners = width // shard
    whole = pl.BlockSpec((tokens, LANES), lambda i: (0, 0))
    return pl.pallas_call(
        lambda *refs: column_kernel(*refs, unroll=min(16, shard // LANES)),
        grid=(width // block,),
        in_specs=[pl.BlockSpec((tokens, block), lambda i: (0, i)), whole, whole, whole],
        out_specs=[pl.BlockSpec((1, 1, shard), lambda i: (i, 0, 0)), whole],
        out_shape=[
            jax.ShapeDtypeStruct((owners, 1, shard), F32),
            jax.ShapeDtypeStruct((tokens, LANES), F32),
        ],
        compiler_params=params(),
        name="column_sums",
    )(teacher, offset, row_here, row_there)


def row_kernel(t_ref, a_ref, c_ref, out_ref, col_ref, *, unroll, balance):
    tokens, block = t_ref.shape
    span = LANES * unroll
    col_ref[...] = balance / c_ref[0]

    @pl.when(pl.program_id(0) == 0)
    def _():
        out_ref[...] = jnp.zeros_like(out_ref)

    def chunk(step, carry):
        base = pl.multiple_of(step * span, span)
        cols = [
            jnp.broadcast_to(col_ref[:, pl.ds(base + j * LANES, LANES)], (GROUP, LANES))
            for j in range(unroll)
        ]
        for r in range(0, tokens, GROUP):
            offset = a_ref[r : r + GROUP, :]
            acc = out_ref[r : r + GROUP, :]
            for j in range(unroll):
                x = t_ref[r : r + GROUP, pl.ds(base + j * LANES, LANES)].astype(F32)
                acc = acc + jnp.exp2(x * TEACH - offset) * cols[j]
            out_ref[r : r + GROUP, :] = acc
        return carry

    lax.fori_loop(0, block // span, chunk, 0)


def row_pass(teacher, offset, sums, balance):
    tokens, width = teacher.shape
    owners, _, block = sums.shape
    whole = pl.BlockSpec((tokens, LANES), lambda i: (0, 0))
    cols = pl.BlockSpec((1, block), lambda i: (0, i))
    return pl.pallas_call(
        lambda *refs: row_kernel(*refs, unroll=min(16, block // LANES), balance=balance),
        grid=(width // block,),
        in_specs=[pl.BlockSpec((tokens, block), lambda i: (0, i)), whole, pl.BlockSpec((1, 1, block), lambda i: (i, 0, 0))],
        out_specs=[whole, cols],
        out_shape=[
            jax.ShapeDtypeStruct((tokens, LANES), F32),
            jax.ShapeDtypeStruct((1, width), F32),
        ],
        compiler_params=params(),
        name="row_sums",
    )(teacher, offset, sums)


def parts_of_left(hi, lo, axis):
    return jnp.concatenate([hi, lo, hi], axis=axis)


def parts_of_right(hi, lo, axis):
    return jnp.concatenate([hi, hi, lo], axis=axis)


def student_kernel(u_ref, w_ref, m_ref, s_ref):
    tokens = u_ref.shape[1]

    @pl.when(pl.program_id(0) == 0)
    def _():
        m_ref[...] = jnp.full_like(m_ref, -1e30)
        s_ref[...] = jnp.zeros_like(s_ref)

    rows = w_ref.shape[0]
    chunk = min(rows, 512)
    largest, total = m_ref[...], s_ref[...]
    scores = []
    for r in range(0, rows, chunk):
        w_hi, w_lo = split(w_ref[r : r + chunk, :])
        logits = dot(parts_of_left(w_hi, w_lo, 1), u_ref[...])
        scores.append(logits.reshape(chunk // 8, 8, tokens))
    for logits in scores:
        best = jnp.maximum(largest, jnp.max(logits, axis=0))
        fresh = jnp.sum(jnp.exp2(logits - best[None]), axis=0)
        total = total * jnp.exp2(largest - best) + fresh
        largest = best
    m_ref[...] = largest
    s_ref[...] = total


def student_pass(u_turned, protos):
    tokens = u_turned.shape[1]
    rows, depth = protos.shape
    block = min(rows, 2048)
    stat = pl.BlockSpec((8, tokens), lambda i: (0, 0))
    shape = jax.ShapeDtypeStruct((8, tokens), F32)
    return pl.pallas_call(
        student_kernel,
        grid=(rows // block,),
        in_specs=[
            pl.BlockSpec(u_turned.shape, lambda i: (0, 0)),
            pl.BlockSpec((block, depth), lambda i: (i, 0)),
        ],
        out_specs=[stat, stat],
        out_shape=[shape, shape],
        compiler_params=params(),
        name="student_stats",
    )(u_turned, protos)


def grad_kernel(own, u_parts, t_parts, lse, offset, tok_in, *refs, blocks, arrivals, parity):
    teach, cols, protos = refs[:blocks], refs[blocks : 2 * blocks], refs[2 * blocks : 3 * blocks]
    arrived = refs[3 * blocks : 3 * blocks + arrivals]
    outs = refs[3 * blocks + arrivals : 4 * blocks + arrivals]
    tok_out = refs[4 * blocks + arrivals]

    @pl.when(pl.program_id(0) == 0)
    def _():
        tok_out[...] = tok_in[...]

    token_part = tok_out[...]
    lse_col = lse[:, :1]
    off_col = offset[:, :1]
    for i in range(blocks):
        w_hi, w_lo = split(protos[i][...])
        logits = dot(u_parts[...], parts_of_right(w_hi, w_lo, 1), ((1,), (1,)))
        student = jnp.exp2(logits - lse_col)
        target = jnp.exp2(teach[i][...].astype(F32) * TEACH - off_col) * cols[i][...]
        g_hi, g_lo = split(student - target)
        part = dot(t_parts[...], parts_of_right(g_hi, g_lo, 0))
        if arrivals == 1:
            odd = own[parity].astype(F32)
            part = part + arrived[0][...] * (odd if i == 0 else 1.0 - odd)
        elif arrivals:
            part = part + arrived[i][...]
        outs[i][...] = part
        token_part = token_part + dot(parts_of_left(g_hi, g_lo, 1), parts_of_right(w_hi, w_lo, 0))
    tok_out[...] = token_part


def grad_step(own, slots, consts, tok, teacher, cols, protos, arrived, width):
    tokens, depth = tok.shape
    block = min(width, 512)
    count = width // block
    blocks = len(slots)

    def whole(shape):
        return pl.BlockSpec(shape, lambda g, own: (0, 0))

    def across(shape):
        return pl.BlockSpec(shape, lambda g, own: (0, g))

    def picked(shape, slot):
        return pl.BlockSpec(shape, lambda g, own: (0, own[slot] * count + g))

    def rows(shape, slot):
        return pl.BlockSpec(shape, lambda g, own: (own[slot] * count + g, 0))

    grid = pltpu.PrefetchScalarGridSpec(
        num_scalar_prefetch=1,
        grid=(count,),
        in_specs=[whole(c.shape) for c in consts]
        + [whole(tok.shape)]
        + [picked((tokens, block), slot) for slot in slots]
        + [picked((1, block), slot) for slot in slots]
        + [rows((block, depth), slot) for slot in slots]
        + [across((depth, block)) for x in arrived],
        out_specs=[across((depth, block)) for slot in slots] + [whole(tok.shape)],
    )
    *parts, tok = pl.pallas_call(
        lambda *refs: grad_kernel(
            *refs, blocks=blocks, arrivals=len(arrived), parity=own.shape[0] - 1
        ),
        grid_spec=grid,
        out_shape=[jax.ShapeDtypeStruct((depth, width), F32) for slot in slots]
        + [jax.ShapeDtypeStruct(tok.shape, F32)],
        compiler_params=params(),
        name="grad_blocks",
    )(
        own,
        *consts,
        tok,
        *([teacher] * blocks),
        *([cols] * blocks),
        *([protos] * blocks),
        *arrived,
    )
    return parts, tok


def proto_kernel(turned_a, turned_b, gain_a, gain_b, *refs):
    grad_ref, gains_ref = refs[6:]
    for i, (turned, gain) in enumerate(((turned_a, gain_a), (turned_b, gain_b))):
        a, b, c = refs[3 * i : 3 * i + 3]
        summed = a[...] + (b[...] + c[...])
        protos = turned[...]
        norm = jnp.sqrt(jnp.sum(protos * protos, axis=0, keepdims=True) + EPS)
        unit = protos / norm
        gain_dot = jnp.sum(unit * summed, axis=0, keepdims=True)
        grad = gain[...] / (TEMP_S * norm) * (summed - unit * gain_dot)
        grad_ref[i] = grad.T
        gains_ref[i] = gain_dot / TEMP_S


def proto_grads(prototypes, gain, parts):
    depth, width = parts[0].shape
    block = min(width, 256)
    count = width // block
    turned = prototypes.T
    gain_row = gain[None, :]

    def at(shape, sub):
        return pl.BlockSpec(shape, lambda i: (0, sub * count + i))

    grad, gains = pl.pallas_call(
        proto_kernel,
        grid=(count,),
        in_specs=[at((depth, block), 0), at((depth, block), 1), at((1, block), 0), at((1, block), 1)]
        + [pl.BlockSpec((depth, block), lambda i: (0, i))] * 6,
        out_specs=[
            pl.BlockSpec((2, block, depth), lambda i: (0, i, 0)),
            pl.BlockSpec((2, 1, block), lambda i: (0, 0, i)),
        ],
        out_shape=[
            jax.ShapeDtypeStruct((2, width, depth), F32),
            jax.ShapeDtypeStruct((2, 1, width), F32),
        ],
        compiler_params=params(),
        name="proto_grads",
    )(turned, turned, gain_row, gain_row, *parts)
    return grad.reshape(2 * width, depth), gains.reshape(2 * width)


def halves(count):
    return [1 << bit for bit in range(count.bit_length() - 1)]


def swap(x, axis, count, distance):
    return lax.ppermute(x, axis, [(i, i ^ distance) for i in range(count)])


def sum_pair(x, axis, count):
    steps = halves(count)
    for distance in steps[:-1]:
        x = x + swap(x, axis, count, distance)
    return x, swap(x, axis, count, steps[-1])


def column_total(x):
    mine = jnp.sum(lax.all_to_all(x, "dp", 0, 0, tiled=True), axis=0, keepdims=True)
    return lax.all_to_all(jnp.broadcast_to(mine, x.shape), "dp", 0, 0, tiled=True)


def log_total(largest, total, axis, count):
    stats = jnp.stack([largest, total])
    for distance in halves(count):
        other = swap(stats, axis, count, distance)
        top = jnp.maximum(stats[0], other[0])
        both = stats[1] * jnp.exp2(stats[0] - top) + other[1] * jnp.exp2(other[0] - top)
        stats = jnp.stack([top, both])
    return stats[0] + jnp.log2(stats[1])


def sublane_stats(largest, total):
    top = jnp.max(largest, axis=0)
    return top, jnp.sum(total * jnp.exp2(largest - top[None, :]), axis=0)


def ring_order(count):
    depth = count // 4
    up = [z * 4 + core for z in range(depth) for core in range(2)]
    down = [z * 4 + 2 + core for z in reversed(range(depth)) for core in range(2)]
    return up + down


def body(packed, crop_offsets, masked_patch, teacher_logits, prototypes, gain):
    tokens_here = masked_patch.shape[0]
    crops_here = crop_offsets.shape[0]
    per_crop = tokens_here // crops_here
    dp_count = lax.axis_size("dp")
    proto_count = lax.axis_size("proto")
    slice_cols = teacher_logits.shape[1]
    shard = prototypes.shape[0]
    total_tokens = tokens_here * dp_count
    total_protos = slice_cols * proto_count
    loss_scale = total_protos / math.sqrt(total_tokens)
    balance = total_tokens / total_protos
    width = shard // 2
    half = dp_count // 2

    order = ring_order(dp_count)
    place = {d: p for p, d in enumerate(order)}

    def around(step):
        return [(d, order[(place[d] + step) % dp_count]) for d in range(dp_count)]

    ahead, behind = around(1), around(-1)
    slot_of = np.zeros((dp_count, 2 * dp_count + 1), np.int32)
    for d in range(dp_count):
        slot_of[d, 2 * dp_count] = place[d] % 2
        for far in range(dp_count):
            for sub in range(2):
                slot_of[d, 2 * far + sub] = 2 * order[(place[d] + far) % dp_count] + sub
    own = jnp.asarray(slot_of)[lax.axis_index("dp")]

    def slot(far, sub):
        return 2 * (far % dp_count) + sub

    proto_norm = jnp.sqrt(jnp.sum(prototypes * prototypes, axis=1, keepdims=True) + EPS)
    unit_proto = prototypes / proto_norm
    weights = unit_proto * (gain / TEMP_S)[:, None]
    gathered = lax.all_gather(weights, "dp", axis=0, tiled=True)

    crop_of = jnp.arange(tokens_here, dtype=jnp.int32) // per_crop
    match = crop_of[:, None] == jnp.arange(crops_here, dtype=jnp.int32)[None, :]
    starts = jnp.sum(jnp.where(match, crop_offsets[None, :], 0), axis=1)
    row_index = starts + masked_patch
    picked = jnp.take(packed, row_index, axis=0)
    inverse = lax.rsqrt(jnp.sum(picked * picked, axis=1, keepdims=True) + EPS)
    unit_tok = picked * inverse

    def pieces(x):
        hi = lax.reduce_precision(x, 8, 7)
        return hi.astype(BF16), (x - hi).astype(BF16)

    u_hi, u_lo = pieces(unit_tok * LOG2E)
    u_parts = parts_of_left(u_hi, u_lo, 1)
    u_turned = parts_of_right(u_hi, u_lo, 1).T
    t_parts = parts_of_left(*pieces(unit_tok.T), 1)

    top, total, teacher_logits = teacher_stats(teacher_logits)
    base = log_total(top[:, 0], jnp.sum(total, axis=1), "proto", proto_count)
    offset = jnp.broadcast_to(base[:, None], (tokens_here, LANES))
    lane = lax.broadcasted_iota(jnp.int32, (tokens_here, LANES), 1)
    row_here = jnp.where(lane == 0, 1.0, 0.0).astype(F32)
    row_there = jnp.zeros((tokens_here, LANES), F32)
    for sweep in range(ITERS):
        sums, offset = column_pass(teacher_logits, offset, row_here, row_there, shard)
        sums = column_total(sums)
        rows, cols = row_pass(teacher_logits, offset, sums, balance)
        row_here, row_there = sum_pair(rows, "proto", proto_count)
    row_sum = jnp.sum(row_here, axis=1) + jnp.sum(row_there, axis=1)
    offset = offset + jnp.log2(row_sum)[:, None]
    cols = cols * loss_scale

    largest, total = student_pass(u_turned, gathered)
    lse = log_total(*sublane_stats(largest, total), "proto", proto_count) - math.log2(loss_scale)
    lse = jnp.broadcast_to(lse[:, None], (tokens_here, LANES))

    token_part = jnp.zeros(unit_tok.shape, F32)
    consts = (u_parts, t_parts, lse, offset)

    def blocks_of(slots, arrived):
        return grad_step(
            own, slots, consts, token_part, teacher_logits, cols, gathered, arrived, width
        )

    crossed = [None, None]
    for sub in range(2):
        (part,), token_part = blocks_of((slot(half, sub),), [])
        crossed[sub] = swap(part, "dp", dp_count, 1)
    waiting = [[crossed[0]], [crossed[1]]]
    for far in range(half - 1, 0, -1):
        for sub in range(2):
            (first, second), token_part = blocks_of((slot(far, sub), slot(-far, sub)), waiting[sub])
            waiting[sub] = [
                lax.ppermute(first, "dp", ahead),
                lax.ppermute(second, "dp", behind),
            ]
    mine, token_part = blocks_of((slot(0, 0), slot(0, 1)), [])
    grad_proto, grad_gain = proto_grads(
        prototypes, gain, [x for sub in range(2) for x in (mine[sub], *waiting[sub])]
    )

    for distance in halves(proto_count):
        token_part = token_part + swap(token_part, "proto", proto_count, distance)
    inner_dot = jnp.sum(unit_tok * token_part, axis=1, keepdims=True)
    input_grad = (token_part - unit_tok * inner_dot) * inverse
    grad_packed = jnp.zeros(packed.shape, F32).at[row_index].set(input_grad)
    return (grad_packed, grad_proto, grad_gain)


def solution(mesh):
    placed = (
        P("dp", None),
        P("dp"),
        P("dp"),
        P("dp", "proto"),
        P(("proto", "dp"), None),
        P(("proto", "dp")),
    )
    return jax.shard_map(
        body,
        mesh=mesh,
        in_specs=placed,
        out_specs=(P("dp", None), P(("proto", "dp"), None), P(("proto", "dp"))),
        check_vma=False,
    )
```

```python
import math

import jax
import jax.numpy as jnp
import numpy as np
from jax import lax
from jax.experimental import pallas as pl
from jax.experimental.pallas import tpu as pltpu
from jax.sharding import PartitionSpec as P

ITERS = 3
TEMP_S = 0.1
TEMP_T = 0.07
EPS = 1e-06
LOG2E = math.log2(math.e)
TEACH = LOG2E / TEMP_T
LANES = 128
GROUP = 16
VMEM_LIMIT = 20 * 1024 * 1024
STUDENT_LIMIT = 44 * 1024 * 1024
F32 = jnp.float32
BF16 = jnp.bfloat16


def params(limit=VMEM_LIMIT):
    return pltpu.CompilerParams(vmem_limit_bytes=limit)


def split(x):
    hi = x.astype(BF16)
    return hi, (x - hi.astype(F32)).astype(BF16)


def dot(a, b, dims=((1,), (0,))):
    return lax.dot_general(a, b, (dims, ((), ())), preferred_element_type=F32)


def teacher_kernel(t_ref, m_ref, s_ref, copy_ref, *, width, unroll):
    copy_ref[...] = t_ref[...]
    span = LANES * unroll
    for r in range(0, t_ref.shape[0], GROUP):

        def largest(step, best):
            base = pl.multiple_of(step * span, span)
            for j in range(unroll):
                x = t_ref[r : r + GROUP, pl.ds(base + j * LANES, LANES)].astype(F32)
                best = jnp.maximum(best, x)
            return best

        best = lax.fori_loop(0, width // span, largest, jnp.full((GROUP, LANES), -jnp.inf, F32))
        top = jnp.broadcast_to(jnp.max(best, axis=1, keepdims=True), (GROUP, LANES)) * TEACH

        def total(step, acc):
            base = pl.multiple_of(step * span, span)
            for j in range(unroll):
                x = t_ref[r : r + GROUP, pl.ds(base + j * LANES, LANES)].astype(F32)
                acc = acc + jnp.exp2(x * TEACH - top)
            return acc

        acc = lax.fori_loop(0, width // span, total, jnp.zeros((GROUP, LANES), F32))
        m_ref[r : r + GROUP, :] = top
        s_ref[r : r + GROUP, :] = acc


def teacher_stats(teacher):
    tokens, width = teacher.shape
    rows = 32
    shape = jax.ShapeDtypeStruct((tokens, LANES), F32)
    spec = pl.BlockSpec((rows, LANES), lambda i: (i, 0))
    return pl.pallas_call(
        lambda *refs: teacher_kernel(*refs, width=width, unroll=16),
        grid=(tokens // rows,),
        in_specs=[pl.BlockSpec((rows, width), lambda i: (i, 0))],
        out_specs=[spec, spec, pl.BlockSpec((rows, width), lambda i: (i, 0))],
        out_shape=[shape, shape, pltpu.VMEM(teacher.shape, teacher.dtype)],
        compiler_params=params(),
        name="teacher_stats",
    )(teacher)


def column_kernel(t_ref, a_ref, r1_ref, r2_ref, out_ref, new_ref, *, unroll):
    tokens, block = t_ref.shape

    @pl.when(pl.program_id(0) == 0)
    def _():
        total = jnp.sum(r1_ref[...], axis=1, keepdims=True) + jnp.sum(r2_ref[...], axis=1, keepdims=True)
        new_ref[...] = a_ref[...] + jnp.broadcast_to(jnp.log(total) * LOG2E, new_ref.shape)

    span = LANES * unroll

    def chunk(step, carry):
        base = pl.multiple_of(step * span, span)
        accs = [jnp.zeros((8, LANES), F32) for _ in range(unroll)]
        for r in range(0, tokens, GROUP):
            offset = new_ref[r : r + GROUP, :]
            for j in range(unroll):
                x = t_ref[r : r + GROUP, pl.ds(base + j * LANES, LANES)].astype(F32)
                e = jnp.exp2(x * TEACH - offset)
                accs[j] = accs[j] + (e[:8] + e[8:])
        for j in range(unroll):
            out_ref[0, :, pl.ds(base + j * LANES, LANES)] = jnp.sum(
                accs[j], axis=0, keepdims=True
            )
        return carry

    lax.fori_loop(0, block // span, chunk, 0)


def column_pass(teacher, offset, row_here, row_there, shard):
    tokens, width = teacher.shape
    block = shard
    owners = width // shard
    whole = pl.BlockSpec((tokens, LANES), lambda i: (0, 0))
    return pl.pallas_call(
        lambda *refs: column_kernel(*refs, unroll=min(16, shard // LANES)),
        grid=(width // block,),
        in_specs=[pl.BlockSpec((tokens, block), lambda i: (0, i)), whole, whole, whole],
        out_specs=[pl.BlockSpec((1, 1, shard), lambda i: (i, 0, 0)), whole],
        out_shape=[
            jax.ShapeDtypeStruct((owners, 1, shard), F32),
            jax.ShapeDtypeStruct((tokens, LANES), F32),
        ],
        compiler_params=params(),
        name="column_sums",
    )(teacher, offset, row_here, row_there)


def row_kernel(t_ref, a_ref, c_ref, out_ref, col_ref, *, unroll, balance):
    tokens, block = t_ref.shape
    span = LANES * unroll
    col_ref[...] = balance / c_ref[0]

    @pl.when(pl.program_id(0) == 0)
    def _():
        out_ref[...] = jnp.zeros_like(out_ref)

    def chunk(step, carry):
        base = pl.multiple_of(step * span, span)
        cols = [
            jnp.broadcast_to(col_ref[:, pl.ds(base + j * LANES, LANES)], (GROUP, LANES))
            for j in range(unroll)
        ]
        for r in range(0, tokens, GROUP):
            offset = a_ref[r : r + GROUP, :]
            acc = out_ref[r : r + GROUP, :]
            for j in range(unroll):
                x = t_ref[r : r + GROUP, pl.ds(base + j * LANES, LANES)].astype(F32)
                acc = acc + jnp.exp2(x * TEACH - offset) * cols[j]
            out_ref[r : r + GROUP, :] = acc
        return carry

    lax.fori_loop(0, block // span, chunk, 0)


def row_pass(teacher, offset, sums, balance):
    tokens, width = teacher.shape
    owners, _, block = sums.shape
    whole = pl.BlockSpec((tokens, LANES), lambda i: (0, 0))
    cols = pl.BlockSpec((1, block), lambda i: (0, i))
    return pl.pallas_call(
        lambda *refs: row_kernel(*refs, unroll=min(16, block // LANES), balance=balance),
        grid=(width // block,),
        in_specs=[pl.BlockSpec((tokens, block), lambda i: (0, i)), whole, pl.BlockSpec((1, 1, block), lambda i: (i, 0, 0))],
        out_specs=[whole, cols],
        out_shape=[
            jax.ShapeDtypeStruct((tokens, LANES), F32),
            jax.ShapeDtypeStruct((1, width), F32),
        ],
        compiler_params=params(),
        name="row_sums",
    )(teacher, offset, sums)


def parts_of_left(hi, lo, axis):
    return jnp.concatenate([hi, lo, hi], axis=axis)


def parts_of_right(hi, lo, axis):
    return jnp.concatenate([hi, hi, lo], axis=axis)


def student_kernel(u_ref, w_ref, m_ref, s_ref, score_a, score_b):
    rows, tokens = score_a.shape
    step = pl.program_id(0)

    def scores(start):
        w_hi, w_lo = split(w_ref[start : start + rows, :])
        return dot(parts_of_left(w_hi, w_lo, 1), u_ref[...])

    def merge(logits, largest, total):
        logits = logits.reshape(rows // 8, 8, tokens)
        best = jnp.maximum(largest, jnp.max(logits, axis=0))
        fresh = jnp.sum(jnp.exp2(logits - best[None]), axis=0)
        return best, total * jnp.exp2(largest - best) + fresh

    @pl.when(step == 0)
    def _():
        m_ref[...] = jnp.full_like(m_ref, -1e30)
        s_ref[...] = jnp.zeros_like(s_ref)
        score_b[...] = jnp.full_like(score_b, -1e30)

    score_a[...] = scores(0)
    stats = merge(score_b[...], m_ref[...], s_ref[...])
    score_b[...] = scores(rows)
    stats = merge(score_a[...], *stats)
    m_ref[...], s_ref[...] = stats

    @pl.when(step == pl.num_programs(0) - 1)
    def _():
        m_ref[...], s_ref[...] = merge(score_b[...], m_ref[...], s_ref[...])


def student_pass(u_turned, protos):
    tokens = u_turned.shape[1]
    rows, depth = protos.shape
    block = min(rows // 2, 4096)
    stat = pl.BlockSpec((8, tokens), lambda i: (0, 0))
    shape = jax.ShapeDtypeStruct((8, tokens), F32)
    return pl.pallas_call(
        student_kernel,
        grid=(rows // block,),
        in_specs=[
            pl.BlockSpec(u_turned.shape, lambda i: (0, 0)),
            pl.BlockSpec((block, depth), lambda i: (i, 0)),
        ],
        out_specs=[stat, stat],
        out_shape=[shape, shape],
        scratch_shapes=[pltpu.VMEM((block // 2, tokens), F32)] * 2,
        compiler_params=params(STUDENT_LIMIT),
        name="student_stats",
    )(u_turned, protos)


def grad_kernel(own, u_parts, t_parts, lse, offset, tok_in, *refs, blocks, arrivals, parity):
    teach, cols, protos = refs[:blocks], refs[blocks : 2 * blocks], refs[2 * blocks : 3 * blocks]
    arrived = refs[3 * blocks : 3 * blocks + arrivals]
    outs = refs[3 * blocks + arrivals : 4 * blocks + arrivals]
    tok_out = refs[4 * blocks + arrivals]

    @pl.when(pl.program_id(0) == 0)
    def _():
        tok_out[...] = tok_in[...]

    token_part = tok_out[...]
    lse_col = lse[:, :1]
    off_col = offset[:, :1]
    for i in range(blocks):
        w_hi, w_lo = split(protos[i][...])
        logits = dot(u_parts[...], parts_of_right(w_hi, w_lo, 1), ((1,), (1,)))
        student = jnp.exp2(logits - lse_col)
        target = jnp.exp2(teach[i][...].astype(F32) * TEACH - off_col) * cols[i][...]
        g_hi, g_lo = split(student - target)
        part = dot(t_parts[...], parts_of_right(g_hi, g_lo, 0))
        if arrivals == 1:
            odd = own[parity].astype(F32)
            part = part + arrived[0][...] * (odd if i == 0 else 1.0 - odd)
        elif arrivals:
            part = part + arrived[i][...]
        outs[i][...] = part
        token_part = token_part + dot(parts_of_left(g_hi, g_lo, 1), parts_of_right(w_hi, w_lo, 0))
    tok_out[...] = token_part


def grad_step(own, slots, consts, tok, teacher, cols, protos, arrived, width):
    tokens, depth = tok.shape
    block = min(width, 512)
    count = width // block
    blocks = len(slots)

    def whole(shape):
        return pl.BlockSpec(shape, lambda g, own: (0, 0))

    def across(shape):
        return pl.BlockSpec(shape, lambda g, own: (0, g))

    def picked(shape, slot):
        return pl.BlockSpec(shape, lambda g, own: (0, own[slot] * count + g))

    def rows(shape, slot):
        return pl.BlockSpec(shape, lambda g, own: (own[slot] * count + g, 0))

    grid = pltpu.PrefetchScalarGridSpec(
        num_scalar_prefetch=1,
        grid=(count,),
        in_specs=[whole(c.shape) for c in consts]
        + [whole(tok.shape)]
        + [picked((tokens, block), slot) for slot in slots]
        + [picked((1, block), slot) for slot in slots]
        + [rows((block, depth), slot) for slot in slots]
        + [across((depth, block)) for x in arrived],
        out_specs=[across((depth, block)) for slot in slots] + [whole(tok.shape)],
    )
    *parts, tok = pl.pallas_call(
        lambda *refs: grad_kernel(
            *refs, blocks=blocks, arrivals=len(arrived), parity=own.shape[0] - 1
        ),
        grid_spec=grid,
        out_shape=[jax.ShapeDtypeStruct((depth, width), F32) for slot in slots]
        + [jax.ShapeDtypeStruct(tok.shape, F32)],
        compiler_params=params(),
        name="grad_blocks",
    )(
        own,
        *consts,
        tok,
        *([teacher] * blocks),
        *([cols] * blocks),
        *([protos] * blocks),
        *arrived,
    )
    return parts, tok


def proto_kernel(turned, gain, a, b, c, *refs):
    grad_ref, gains_ref = refs[-2:]
    summed = a[...] + (b[...] + c[...])
    protos = turned[...]
    norm = jnp.sqrt(jnp.sum(protos * protos, axis=0, keepdims=True) + EPS)
    unit = protos / norm
    gain_dot = jnp.sum(unit * summed, axis=0, keepdims=True)
    grad = gain[...] / (TEMP_S * norm) * (summed - unit * gain_dot)
    grad_ref[...] = grad.T
    gains_ref[...] = gain_dot / TEMP_S


def proto_grads(turned, gain_row, parts, half, done):
    depth, width = parts[0].shape
    block = min(width, 256)
    count = width // block
    return pl.pallas_call(
        proto_kernel,
        grid=(count,),
        in_specs=[
            pl.BlockSpec((depth, block), lambda i: (0, half * count + i)),
            pl.BlockSpec((1, block), lambda i: (0, half * count + i)),
        ]
        + [pl.BlockSpec((depth, block), lambda i: (0, i))] * 3
        + [pl.BlockSpec(memory_space=pl.ANY)] * len(done),
        out_specs=[
            pl.BlockSpec((block, depth), lambda i: (half * count + i, 0)),
            pl.BlockSpec((1, block), lambda i: (0, half * count + i)),
        ],
        out_shape=[
            jax.ShapeDtypeStruct((2 * width, depth), F32),
            jax.ShapeDtypeStruct((1, 2 * width), F32),
        ],
        input_output_aliases={5 + i: i for i in range(len(done))},
        compiler_params=params(),
        name="proto_grads",
    )(turned, gain_row, *parts, *done)


def halves(count):
    return [1 << bit for bit in range(count.bit_length() - 1)]


def swap(x, axis, count, distance):
    return lax.ppermute(x, axis, [(i, i ^ distance) for i in range(count)])


def sum_pair(x, axis, count):
    steps = halves(count)
    for distance in steps[:-1]:
        x = x + swap(x, axis, count, distance)
    return x, swap(x, axis, count, steps[-1])


def column_total(x):
    mine = jnp.sum(lax.all_to_all(x, "dp", 0, 0, tiled=True), axis=0, keepdims=True)
    return lax.all_to_all(jnp.broadcast_to(mine, x.shape), "dp", 0, 0, tiled=True)


def log_total(largest, total, axis, count):
    stats = jnp.stack([largest, total])
    for distance in halves(count):
        other = swap(stats, axis, count, distance)
        top = jnp.maximum(stats[0], other[0])
        both = stats[1] * jnp.exp2(stats[0] - top) + other[1] * jnp.exp2(other[0] - top)
        stats = jnp.stack([top, both])
    return stats[0] + jnp.log2(stats[1])


def sublane_stats(largest, total):
    top = jnp.max(largest, axis=0)
    return top, jnp.sum(total * jnp.exp2(largest - top[None, :]), axis=0)


def ring_order(count):
    depth = count // 4
    up = [z * 4 + core for z in range(depth) for core in range(2)]
    down = [z * 4 + 2 + core for z in reversed(range(depth)) for core in range(2)]
    return up + down


def body(packed, crop_offsets, masked_patch, teacher_logits, prototypes, gain):
    tokens_here = masked_patch.shape[0]
    crops_here = crop_offsets.shape[0]
    per_crop = tokens_here // crops_here
    dp_count = lax.axis_size("dp")
    proto_count = lax.axis_size("proto")
    slice_cols = teacher_logits.shape[1]
    shard = prototypes.shape[0]
    total_tokens = tokens_here * dp_count
    total_protos = slice_cols * proto_count
    loss_scale = total_protos / math.sqrt(total_tokens)
    balance = total_tokens / total_protos
    width = shard // 2
    half = dp_count // 2

    order = ring_order(dp_count)
    place = {d: p for p, d in enumerate(order)}

    def around(step):
        return [(d, order[(place[d] + step) % dp_count]) for d in range(dp_count)]

    ahead, behind = around(1), around(-1)
    slot_of = np.zeros((dp_count, 2 * dp_count + 1), np.int32)
    for d in range(dp_count):
        slot_of[d, 2 * dp_count] = place[d] % 2
        for far in range(dp_count):
            for sub in range(2):
                slot_of[d, 2 * far + sub] = 2 * order[(place[d] + far) % dp_count] + sub
    own = jnp.asarray(slot_of)[lax.axis_index("dp")]

    def slot(far, sub):
        return 2 * (far % dp_count) + sub

    proto_norm = jnp.sqrt(jnp.sum(prototypes * prototypes, axis=1, keepdims=True) + EPS)
    unit_proto = prototypes / proto_norm
    weights = unit_proto * (gain / TEMP_S)[:, None]
    gathered = lax.all_gather(weights, "dp", axis=0, tiled=True)

    crop_of = jnp.arange(tokens_here, dtype=jnp.int32) // per_crop
    match = crop_of[:, None] == jnp.arange(crops_here, dtype=jnp.int32)[None, :]
    starts = jnp.sum(jnp.where(match, crop_offsets[None, :], 0), axis=1)
    row_index = starts + masked_patch
    picked = jnp.take(packed, row_index, axis=0)
    inverse = lax.rsqrt(jnp.sum(picked * picked, axis=1, keepdims=True) + EPS)
    unit_tok = picked * inverse

    def pieces(x):
        hi = lax.reduce_precision(x, 8, 7)
        return hi.astype(BF16), (x - hi).astype(BF16)

    u_hi, u_lo = pieces(unit_tok * LOG2E)
    u_parts = parts_of_left(u_hi, u_lo, 1)
    u_turned = parts_of_right(u_hi, u_lo, 1).T
    t_parts = parts_of_left(*pieces(unit_tok.T), 1)

    top, total, teacher_logits = teacher_stats(teacher_logits)
    base = log_total(top[:, 0], jnp.sum(total, axis=1), "proto", proto_count)
    offset = jnp.broadcast_to(base[:, None], (tokens_here, LANES))
    lane = lax.broadcasted_iota(jnp.int32, (tokens_here, LANES), 1)
    row_here = jnp.where(lane == 0, 1.0, 0.0).astype(F32)
    row_there = jnp.zeros((tokens_here, LANES), F32)
    for sweep in range(ITERS):
        sums, offset = column_pass(teacher_logits, offset, row_here, row_there, shard)
        sums = column_total(sums)
        rows, cols = row_pass(teacher_logits, offset, sums, balance)
        row_here, row_there = sum_pair(rows, "proto", proto_count)
    row_sum = jnp.sum(row_here, axis=1) + jnp.sum(row_there, axis=1)
    offset = offset + jnp.log2(row_sum)[:, None]
    cols = cols * loss_scale

    largest, total = student_pass(u_turned, gathered)
    lse = log_total(*sublane_stats(largest, total), "proto", proto_count) - math.log2(loss_scale)
    lse = jnp.broadcast_to(lse[:, None], (tokens_here, LANES))

    token_part = jnp.zeros(unit_tok.shape, F32)
    consts = (u_parts, t_parts, lse, offset)

    def blocks_of(slots, arrived):
        return grad_step(
            own, slots, consts, token_part, teacher_logits, cols, gathered, arrived, width
        )

    crossed = [None, None]
    for sub in range(2):
        (part,), token_part = blocks_of((slot(half, sub),), [])
        crossed[sub] = swap(part, "dp", dp_count, 1)
    waiting = [[crossed[0]], [crossed[1]]]
    mine = []
    for far in range(half - 1, 0, -1):
        if len(mine) < 2 and far <= half // 2 + 1:
            (part,), token_part = blocks_of((slot(0, len(mine)),), [])
            mine.append(part)
        for sub in range(2):
            (first, second), token_part = blocks_of((slot(far, sub), slot(-far, sub)), waiting[sub])
            waiting[sub] = [
                lax.ppermute(first, "dp", ahead),
                lax.ppermute(second, "dp", behind),
            ]
    turned, gain_row = prototypes.T, gain[None, :]
    grads = ()
    for sub in range(2):
        grads = proto_grads(turned, gain_row, [mine[sub], *waiting[sub]], sub, grads)
    grad_proto, grad_gain = grads[0], grads[1].reshape(shard)

    for distance in halves(proto_count):
        token_part = token_part + swap(token_part, "proto", proto_count, distance)
    inner_dot = jnp.sum(unit_tok * token_part, axis=1, keepdims=True)
    input_grad = (token_part - unit_tok * inner_dot) * inverse
    grad_packed = jnp.zeros(packed.shape, F32).at[row_index].set(input_grad)
    return (grad_packed, grad_proto, grad_gain)


def solution(mesh):
    placed = (
        P("dp", None),
        P("dp"),
        P("dp"),
        P("dp", "proto"),
        P(("proto", "dp"), None),
        P(("proto", "dp")),
    )
    return jax.shard_map(
        body,
        mesh=mesh,
        in_specs=placed,
        out_specs=(P("dp", None), P(("proto", "dp"), None), P(("proto", "dp"))),
        check_vma=False,
    )
```

```python
import math

import jax
import jax.numpy as jnp
import numpy as np
from jax import lax
from jax.experimental import pallas as pl
from jax.experimental.pallas import tpu as pltpu
from jax.sharding import PartitionSpec as P

ITERS = 3
TEMP_S = 0.1
TEMP_T = 0.07
EPS = 1e-06
LOG2E = math.log2(math.e)
TEACH = LOG2E / TEMP_T
LANES = 128
GROUP = 16
VMEM_LIMIT = 20 * 1024 * 1024
STREAM_LIMIT = 52 * 1024 * 1024
F32 = jnp.float32
BF16 = jnp.bfloat16


def params(limit=VMEM_LIMIT):
    return pltpu.CompilerParams(vmem_limit_bytes=limit)


def split(x):
    hi = x.astype(BF16)
    return hi, (x - hi.astype(F32)).astype(BF16)


def dot(a, b, dims=((1,), (0,))):
    return lax.dot_general(a, b, (dims, ((), ())), preferred_element_type=F32)


def teacher_kernel(t_ref, m_ref, s_ref, *, width, unroll):
    span = LANES * unroll
    for r in range(0, t_ref.shape[0], GROUP):

        def largest(step, best):
            base = pl.multiple_of(step * span, span)
            for j in range(unroll):
                x = t_ref[r : r + GROUP, pl.ds(base + j * LANES, LANES)].astype(F32)
                best = jnp.maximum(best, x)
            return best

        best = lax.fori_loop(0, width // span, largest, jnp.full((GROUP, LANES), -jnp.inf, F32))
        top = jnp.broadcast_to(jnp.max(best, axis=1, keepdims=True), (GROUP, LANES)) * TEACH

        def total(step, acc):
            base = pl.multiple_of(step * span, span)
            for j in range(unroll):
                x = t_ref[r : r + GROUP, pl.ds(base + j * LANES, LANES)].astype(F32)
                acc = acc + jnp.exp2(x * TEACH - top)
            return acc

        acc = lax.fori_loop(0, width // span, total, jnp.zeros((GROUP, LANES), F32))
        m_ref[r : r + GROUP, :] = top
        s_ref[r : r + GROUP, :] = acc


def teacher_stats(teacher):
    tokens, width = teacher.shape
    rows = 32
    shape = jax.ShapeDtypeStruct((tokens, LANES), F32)
    spec = pl.BlockSpec((rows, LANES), lambda i: (i, 0))
    return pl.pallas_call(
        lambda *refs: teacher_kernel(*refs, width=width, unroll=16),
        grid=(tokens // rows,),
        in_specs=[pl.BlockSpec((rows, width), lambda i: (i, 0))],
        out_specs=[spec, spec],
        out_shape=[shape, shape],
        compiler_params=params(STREAM_LIMIT),
        name="teacher_stats",
    )(teacher)


def column_kernel(t_ref, a_ref, r1_ref, r2_ref, out_ref, new_ref, *, unroll):
    tokens, block = t_ref.shape

    @pl.when(pl.program_id(0) == 0)
    def _():
        total = jnp.sum(r1_ref[...], axis=1, keepdims=True) + jnp.sum(r2_ref[...], axis=1, keepdims=True)
        new_ref[...] = a_ref[...] + jnp.broadcast_to(jnp.log(total) * LOG2E, new_ref.shape)

    span = LANES * unroll

    def chunk(step, carry):
        base = pl.multiple_of(step * span, span)
        accs = [jnp.zeros((8, LANES), F32) for _ in range(unroll)]
        for r in range(0, tokens, GROUP):
            offset = new_ref[r : r + GROUP, :]
            for j in range(unroll):
                x = t_ref[r : r + GROUP, pl.ds(base + j * LANES, LANES)].astype(F32)
                e = jnp.exp2(x * TEACH - offset)
                accs[j] = accs[j] + (e[:8] + e[8:])
        for j in range(unroll):
            out_ref[0, :, pl.ds(base + j * LANES, LANES)] = jnp.sum(
                accs[j], axis=0, keepdims=True
            )
        return carry

    lax.fori_loop(0, block // span, chunk, 0)


def column_pass(teacher, offset, row_here, row_there, shard):
    tokens, width = teacher.shape
    block = shard
    owners = width // shard
    whole = pl.BlockSpec((tokens, LANES), lambda i: (0, 0))
    return pl.pallas_call(
        lambda *refs: column_kernel(*refs, unroll=min(16, shard // LANES)),
        grid=(width // block,),
        in_specs=[pl.BlockSpec((tokens, block), lambda i: (0, i)), whole, whole, whole],
        out_specs=[pl.BlockSpec((1, 1, shard), lambda i: (i, 0, 0)), whole],
        out_shape=[
            jax.ShapeDtypeStruct((owners, 1, shard), F32),
            jax.ShapeDtypeStruct((tokens, LANES), F32),
        ],
        compiler_params=params(STREAM_LIMIT),
        name="column_sums",
    )(teacher, offset, row_here, row_there)


def row_kernel(t_ref, a_ref, c_ref, out_ref, col_ref, *, unroll, balance):
    tokens, block = t_ref.shape
    span = LANES * unroll
    col_ref[...] = balance / c_ref[0]

    @pl.when(pl.program_id(0) == 0)
    def _():
        out_ref[...] = jnp.zeros_like(out_ref)

    def chunk(step, carry):
        base = pl.multiple_of(step * span, span)
        cols = [
            jnp.broadcast_to(col_ref[:, pl.ds(base + j * LANES, LANES)], (GROUP, LANES))
            for j in range(unroll)
        ]
        for r in range(0, tokens, GROUP):
            offset = a_ref[r : r + GROUP, :]
            acc = out_ref[r : r + GROUP, :]
            for j in range(unroll):
                x = t_ref[r : r + GROUP, pl.ds(base + j * LANES, LANES)].astype(F32)
                acc = acc + jnp.exp2(x * TEACH - offset) * cols[j]
            out_ref[r : r + GROUP, :] = acc
        return carry

    lax.fori_loop(0, block // span, chunk, 0)


def row_pass(teacher, offset, sums, balance):
    tokens, width = teacher.shape
    owners, _, block = sums.shape
    whole = pl.BlockSpec((tokens, LANES), lambda i: (0, 0))
    cols = pl.BlockSpec((1, block), lambda i: (0, i))
    return pl.pallas_call(
        lambda *refs: row_kernel(*refs, unroll=min(16, block // LANES), balance=balance),
        grid=(width // block,),
        in_specs=[pl.BlockSpec((tokens, block), lambda i: (0, i)), whole, pl.BlockSpec((1, 1, block), lambda i: (i, 0, 0))],
        out_specs=[whole, cols],
        out_shape=[
            jax.ShapeDtypeStruct((tokens, LANES), F32),
            jax.ShapeDtypeStruct((1, width), F32),
        ],
        compiler_params=params(STREAM_LIMIT),
        name="row_sums",
    )(teacher, offset, sums)


def parts_of_left(hi, lo, axis):
    return jnp.concatenate([hi, lo, hi], axis=axis)


def parts_of_right(hi, lo, axis):
    return jnp.concatenate([hi, hi, lo], axis=axis)


def student_kernel(u_ref, w_ref, m_ref, s_ref, score_a, score_b):
    rows, tokens = score_a.shape
    held = (score_b, score_a)
    step = pl.program_id(0)

    def scores(start):
        w_hi, w_lo = split(w_ref[start : start + rows, :])
        return dot(parts_of_left(w_hi, w_lo, 1), u_ref[...])

    def merge(logits, largest, total):
        logits = logits.reshape(rows // 8, 8, tokens)
        best = jnp.maximum(largest, jnp.max(logits, axis=0))
        fresh = jnp.sum(jnp.exp2(logits - best[None]), axis=0)
        return best, total * jnp.exp2(largest - best) + fresh

    @pl.when(step == 0)
    def _():
        m_ref[...] = jnp.full_like(m_ref, -1e30)
        s_ref[...] = jnp.zeros_like(s_ref)
        score_b[...] = jnp.full_like(score_b, -1e30)

    stats = m_ref[...], s_ref[...]
    pieces = w_ref.shape[0] // rows
    for i in range(pieces):
        held[(i + 1) % 2][...] = scores(i * rows)
        stats = merge(held[i % 2][...], *stats)
    m_ref[...], s_ref[...] = stats

    @pl.when(step == pl.num_programs(0) - 1)
    def _():
        m_ref[...], s_ref[...] = merge(score_b[...], m_ref[...], s_ref[...])


def student_pass(u_turned, protos):
    tokens = u_turned.shape[1]
    rows, depth = protos.shape
    block = min(rows // 2, 4096)
    stat = pl.BlockSpec((8, tokens), lambda i: (0, 0))
    shape = jax.ShapeDtypeStruct((8, tokens), F32)
    return pl.pallas_call(
        student_kernel,
        grid=(rows // block,),
        in_specs=[
            pl.BlockSpec(u_turned.shape, lambda i: (0, 0)),
            pl.BlockSpec((block, depth), lambda i: (i, 0)),
        ],
        out_specs=[stat, stat],
        out_shape=[shape, shape],
        scratch_shapes=[pltpu.VMEM((min(block // 2, 512), tokens), F32)] * 2,
        compiler_params=params(STREAM_LIMIT),
        name="student_stats",
    )(u_turned, protos)


def grad_kernel(own, u_parts, t_parts, lse, offset, tok_in, *refs, blocks, arrivals, parity):
    teach, cols, protos = refs[:blocks], refs[blocks : 2 * blocks], refs[2 * blocks : 3 * blocks]
    arrived = refs[3 * blocks : 3 * blocks + arrivals]
    outs = refs[3 * blocks + arrivals : 4 * blocks + arrivals]
    tok_out = refs[4 * blocks + arrivals]

    @pl.when(pl.program_id(0) == 0)
    def _():
        tok_out[...] = tok_in[...]

    token_part = tok_out[...]
    lse_col = lse[:, :1]
    off_col = offset[:, :1]
    for i in range(blocks):
        w_hi, w_lo = split(protos[i][...])
        logits = dot(u_parts[...], parts_of_right(w_hi, w_lo, 1), ((1,), (1,)))
        student = jnp.exp2(logits - lse_col)
        target = jnp.exp2(teach[i][...].astype(F32) * TEACH - off_col) * cols[i][...]
        g_hi, g_lo = split(student - target)
        part = dot(t_parts[...], parts_of_right(g_hi, g_lo, 0))
        if arrivals == 1:
            odd = own[parity].astype(F32)
            part = part + arrived[0][...] * (odd if i == 0 else 1.0 - odd)
        elif arrivals:
            part = part + arrived[i][...]
        outs[i][...] = part
        token_part = token_part + dot(parts_of_left(g_hi, g_lo, 1), parts_of_right(w_hi, w_lo, 0))
    tok_out[...] = token_part


def grad_step(own, slots, consts, tok, teacher, cols, protos, arrived, width, limit):
    tokens, depth = tok.shape
    block = min(width, 512)
    count = width // block
    blocks = len(slots)

    def whole(shape):
        return pl.BlockSpec(shape, lambda g, own: (0, 0))

    def across(shape):
        return pl.BlockSpec(shape, lambda g, own: (0, g))

    def picked(shape, slot):
        return pl.BlockSpec(shape, lambda g, own: (0, own[slot] * count + g))

    def rows(shape, slot):
        return pl.BlockSpec(shape, lambda g, own: (own[slot] * count + g, 0))

    grid = pltpu.PrefetchScalarGridSpec(
        num_scalar_prefetch=1,
        grid=(count,),
        in_specs=[whole(c.shape) for c in consts]
        + [whole(tok.shape)]
        + [picked((tokens, block), slot) for slot in slots]
        + [picked((1, block), slot) for slot in slots]
        + [rows((block, depth), slot) for slot in slots]
        + [across((depth, block)) for x in arrived],
        out_specs=[across((depth, block)) for slot in slots] + [whole(tok.shape)],
    )
    *parts, tok = pl.pallas_call(
        lambda *refs: grad_kernel(
            *refs, blocks=blocks, arrivals=len(arrived), parity=own.shape[0] - 1
        ),
        grid_spec=grid,
        out_shape=[jax.ShapeDtypeStruct((depth, width), F32) for slot in slots]
        + [jax.ShapeDtypeStruct(tok.shape, F32)],
        compiler_params=params(limit),
        name="grad_blocks",
    )(
        own,
        *consts,
        tok,
        *([teacher] * blocks),
        *([cols] * blocks),
        *([protos] * blocks),
        *arrived,
    )
    return parts, tok


def proto_kernel(turned, gain, a, b, c, *refs):
    grad_ref, gains_ref = refs[-2:]
    summed = a[...] + (b[...] + c[...])
    protos = turned[...]
    norm = jnp.sqrt(jnp.sum(protos * protos, axis=0, keepdims=True) + EPS)
    unit = protos / norm
    gain_dot = jnp.sum(unit * summed, axis=0, keepdims=True)
    grad = gain[...] / (TEMP_S * norm) * (summed - unit * gain_dot)
    grad_ref[...] = grad.T
    gains_ref[...] = gain_dot / TEMP_S


def proto_grads(turned, gain_row, parts, half, done):
    depth, width = parts[0].shape
    block = min(width, 512)
    count = width // block
    return pl.pallas_call(
        proto_kernel,
        grid=(count,),
        in_specs=[
            pl.BlockSpec((depth, block), lambda i: (0, half * count + i)),
            pl.BlockSpec((1, block), lambda i: (0, half * count + i)),
        ]
        + [pl.BlockSpec((depth, block), lambda i: (0, i))] * 3
        + [pl.BlockSpec(memory_space=pl.ANY)] * len(done),
        out_specs=[
            pl.BlockSpec((block, depth), lambda i: (half * count + i, 0)),
            pl.BlockSpec((1, block), lambda i: (0, half * count + i)),
        ],
        out_shape=[
            jax.ShapeDtypeStruct((2 * width, depth), F32),
            jax.ShapeDtypeStruct((1, 2 * width), F32),
        ],
        input_output_aliases={5 + i: i for i in range(len(done))},
        compiler_params=params(),
        name="proto_grads",
    )(turned, gain_row, *parts, *done)


def token_kernel(here, there, unit, inverse, after, out):
    token_sum = here[...] + there[...]
    inner = jnp.sum(unit[...] * token_sum, axis=1, keepdims=True)
    out[...] = (token_sum - unit[...] * inner) * inverse[...][:, :1]


def token_grads(here, there, unit, inverse, after):
    vmem = pl.BlockSpec(memory_space=pltpu.VMEM)
    return pl.pallas_call(
        token_kernel,
        in_specs=[vmem] * 4 + [pl.BlockSpec(memory_space=pl.ANY)],
        out_specs=vmem,
        out_shape=jax.ShapeDtypeStruct(unit.shape, F32),
        compiler_params=params(),
        name="token_grads",
    )(here, there, unit, inverse, after)


def halves(count):
    return [1 << bit for bit in range(count.bit_length() - 1)]


def swap(x, axis, count, distance):
    return lax.ppermute(x, axis, [(i, i ^ distance) for i in range(count)])


def sum_pair(x, axis, count):
    steps = halves(count)
    for distance in steps[:-1]:
        x = x + swap(x, axis, count, distance)
    return x, swap(x, axis, count, steps[-1])


def column_total(x):
    mine = jnp.sum(lax.all_to_all(x, "dp", 0, 0, tiled=True), axis=0, keepdims=True)
    return lax.all_to_all(jnp.broadcast_to(mine, x.shape), "dp", 0, 0, tiled=True)


def log_total(largest, total, axis, count):
    stats = jnp.stack([largest, total])
    for distance in halves(count):
        other = swap(stats, axis, count, distance)
        top = jnp.maximum(stats[0], other[0])
        both = stats[1] * jnp.exp2(stats[0] - top) + other[1] * jnp.exp2(other[0] - top)
        stats = jnp.stack([top, both])
    return stats[0] + jnp.log2(stats[1])


def sublane_stats(largest, total):
    top = jnp.max(largest, axis=0)
    return top, jnp.sum(total * jnp.exp2(largest - top[None, :]), axis=0)


def ring_order(count):
    depth = count // 4
    up = [z * 4 + core for z in range(depth) for core in range(2)]
    down = [z * 4 + 2 + core for z in reversed(range(depth)) for core in range(2)]
    return up + down


def body(packed, crop_offsets, masked_patch, teacher_logits, prototypes, gain):
    tokens_here = masked_patch.shape[0]
    crops_here = crop_offsets.shape[0]
    per_crop = tokens_here // crops_here
    dp_count = lax.axis_size("dp")
    proto_count = lax.axis_size("proto")
    slice_cols = teacher_logits.shape[1]
    shard = prototypes.shape[0]
    total_tokens = tokens_here * dp_count
    total_protos = slice_cols * proto_count
    loss_scale = total_protos / math.sqrt(total_tokens)
    balance = total_tokens / total_protos
    width = shard // 2
    half = dp_count // 2

    order = ring_order(dp_count)
    place = {d: p for p, d in enumerate(order)}

    def around(step):
        return [(d, order[(place[d] + step) % dp_count]) for d in range(dp_count)]

    ahead, behind = around(1), around(-1)
    slot_of = np.zeros((dp_count, 2 * dp_count + 1), np.int32)
    for d in range(dp_count):
        slot_of[d, 2 * dp_count] = place[d] % 2
        for far in range(dp_count):
            for sub in range(2):
                slot_of[d, 2 * far + sub] = 2 * order[(place[d] + far) % dp_count] + sub
    own = jnp.asarray(slot_of)[lax.axis_index("dp")]

    def slot(far, sub):
        return 2 * (far % dp_count) + sub

    proto_norm = jnp.sqrt(jnp.sum(prototypes * prototypes, axis=1, keepdims=True) + EPS)
    unit_proto = prototypes / proto_norm
    weights = unit_proto * (gain / TEMP_S)[:, None]
    gathered = lax.all_gather(weights, "dp", axis=0, tiled=True)

    crop_of = jnp.arange(tokens_here, dtype=jnp.int32) // per_crop
    match = crop_of[:, None] == jnp.arange(crops_here, dtype=jnp.int32)[None, :]
    starts = jnp.sum(jnp.where(match, crop_offsets[None, :], 0), axis=1)
    row_index = starts + masked_patch
    picked = jnp.take(packed, row_index, axis=0)
    inverse = lax.rsqrt(jnp.sum(picked * picked, axis=1, keepdims=True) + EPS)
    unit_tok = picked * inverse

    def pieces(x):
        hi = lax.reduce_precision(x, 8, 7)
        return hi.astype(BF16), (x - hi).astype(BF16)

    u_hi, u_lo = pieces(unit_tok * LOG2E)
    u_parts = parts_of_left(u_hi, u_lo, 1)
    u_turned = parts_of_right(u_hi, u_lo, 1).T
    t_parts = parts_of_left(*pieces(unit_tok.T), 1)

    top, total = teacher_stats(teacher_logits)
    base = log_total(top[:, 0], jnp.sum(total, axis=1), "proto", proto_count)
    offset = jnp.broadcast_to(base[:, None], (tokens_here, LANES))
    lane = lax.broadcasted_iota(jnp.int32, (tokens_here, LANES), 1)
    row_here = jnp.where(lane == 0, 1.0, 0.0).astype(F32)
    row_there = jnp.zeros((tokens_here, LANES), F32)
    for sweep in range(ITERS):
        sums, offset = column_pass(teacher_logits, offset, row_here, row_there, shard)
        sums = column_total(sums)
        rows, cols = row_pass(teacher_logits, offset, sums, balance)
        row_here, row_there = sum_pair(rows, "proto", proto_count)
    row_sum = jnp.sum(row_here, axis=1) + jnp.sum(row_there, axis=1)
    offset = offset + jnp.log2(row_sum)[:, None]
    cols = cols * loss_scale

    largest, total = student_pass(u_turned, gathered)
    lse = log_total(*sublane_stats(largest, total), "proto", proto_count) - math.log2(loss_scale)
    lse = jnp.broadcast_to(lse[:, None], (tokens_here, LANES))

    token_part = jnp.zeros(unit_tok.shape, F32)
    consts = (u_parts, t_parts, lse, offset)

    def blocks_of(slots, arrived, limit=VMEM_LIMIT):
        return grad_step(
            own, slots, consts, token_part, teacher_logits, cols, gathered, arrived, width, limit
        )

    crossed = [None, None]
    for sub in range(2):
        (part,), token_part = blocks_of((slot(half, sub),), [], STREAM_LIMIT)
        crossed[sub] = swap(part, "dp", dp_count, 1)
    waiting = [[crossed[0]], [crossed[1]]]
    mine = []
    for far in range(half - 1, 0, -1):
        if len(mine) < 2 and far <= half // 2 + 1:
            (part,), token_part = blocks_of((slot(0, len(mine)),), [])
            mine.append(part)
        for sub in range(2):
            (first, second), token_part = blocks_of(
                (slot(far, sub), slot(-far, sub)),
                waiting[sub],
                STREAM_LIMIT if far == half - 1 else VMEM_LIMIT,
            )
            waiting[sub] = [
                lax.ppermute(first, "dp", ahead),
                lax.ppermute(second, "dp", behind),
            ]
    token_here, token_there = sum_pair(token_part, "proto", proto_count)
    turned, gain_row = prototypes.T, gain[None, :]
    grads = proto_grads(turned, gain_row, [mine[0], *waiting[0]], 0, ())
    input_grad = token_grads(
        token_here,
        token_there,
        unit_tok,
        jnp.broadcast_to(inverse, (tokens_here, LANES)),
        grads[1],
    )
    grads = proto_grads(turned, gain_row, [mine[1], *waiting[1]], 1, grads)
    grad_proto, grad_gain = grads[0], grads[1].reshape(shard)
    grad_packed = jnp.zeros(packed.shape, F32).at[row_index].set(input_grad)
    return (grad_packed, grad_proto, grad_gain)


def solution(mesh):
    placed = (
        P("dp", None),
        P("dp"),
        P("dp"),
        P("dp", "proto"),
        P(("proto", "dp"), None),
        P(("proto", "dp")),
    )
    return jax.shard_map(
        body,
        mesh=mesh,
        in_specs=placed,
        out_specs=(P("dp", None), P(("proto", "dp"), None), P(("proto", "dp"))),
        check_vma=False,
    )
```

```python
import math

import jax
import jax.numpy as jnp
import numpy as np
from jax import lax
from jax.experimental import pallas as pl
from jax.experimental.pallas import tpu as pltpu
from jax.sharding import PartitionSpec as P

ITERS = 3
TEMP_S = 0.1
TEMP_T = 0.07
EPS = 1e-06
LOG2E = math.log2(math.e)
TEACH = LOG2E / TEMP_T
LANES = 128
GROUP = 16
VMEM_LIMIT = 20 * 1024 * 1024
STREAM_LIMIT = 52 * 1024 * 1024
F32 = jnp.float32
BF16 = jnp.bfloat16


def params(limit=VMEM_LIMIT):
    return pltpu.CompilerParams(vmem_limit_bytes=limit)


def teacher_block(teacher, buf, sems):
    count, _, block = buf.shape
    step = pl.program_id(0)

    def fetch(i, start):
        return pltpu.make_async_copy(
            teacher.at[:, pl.ds(start, block)], buf.at[i], sems.at[i]
        )

    @pl.when(step == 0)
    def _():
        for i in range(count):
            fetch(i, i * block).start()

    fetch(step, pl.multiple_of(step * block, LANES)).wait()
    return buf.at[step]


def teacher_scratch(teacher, block):
    tokens, width = teacher.shape
    count = width // block
    return [pltpu.VMEM((count, tokens, block), teacher.dtype), pltpu.SemaphoreType.DMA((count,))]


def in_hbm(x):
    return pltpu.with_memory_space_constraint(x, pltpu.HBM)


def split(x):
    hi = x.astype(BF16)
    return hi, (x - hi.astype(F32)).astype(BF16)


def dot(a, b, dims=((1,), (0,))):
    return lax.dot_general(a, b, (dims, ((), ())), preferred_element_type=F32)


def teacher_kernel(t_ref, m_ref, s_ref, *, width, unroll):
    span = LANES * unroll
    for r in range(0, t_ref.shape[0], GROUP):

        def largest(step, best):
            base = pl.multiple_of(step * span, span)
            for j in range(unroll):
                x = t_ref[r : r + GROUP, pl.ds(base + j * LANES, LANES)].astype(F32)
                best = jnp.maximum(best, x)
            return best

        best = lax.fori_loop(0, width // span, largest, jnp.full((GROUP, LANES), -jnp.inf, F32))
        top = jnp.broadcast_to(jnp.max(best, axis=1, keepdims=True), (GROUP, LANES)) * TEACH

        def total(step, acc):
            base = pl.multiple_of(step * span, span)
            for j in range(unroll):
                x = t_ref[r : r + GROUP, pl.ds(base + j * LANES, LANES)].astype(F32)
                acc = acc + jnp.exp2(x * TEACH - top)
            return acc

        acc = lax.fori_loop(0, width // span, total, jnp.zeros((GROUP, LANES), F32))
        m_ref[r : r + GROUP, :] = top
        s_ref[r : r + GROUP, :] = acc


def teacher_stats(teacher):
    tokens, width = teacher.shape
    rows = 32
    shape = jax.ShapeDtypeStruct((tokens, LANES), F32)
    spec = pl.BlockSpec((rows, LANES), lambda i: (i, 0))
    return pl.pallas_call(
        lambda *refs: teacher_kernel(*refs, width=width, unroll=16),
        grid=(tokens // rows,),
        in_specs=[pl.BlockSpec((rows, width), lambda i: (i, 0))],
        out_specs=[spec, spec],
        out_shape=[shape, shape],
        compiler_params=params(STREAM_LIMIT),
        name="teacher_stats",
    )(in_hbm(teacher))


def column_kernel(teacher, a_ref, r1_ref, r2_ref, out_ref, new_ref, buf, sems, *, unroll):
    t_ref = teacher_block(teacher, buf, sems)
    tokens, block = t_ref.shape

    @pl.when(pl.program_id(0) == 0)
    def _():
        total = jnp.sum(r1_ref[...], axis=1, keepdims=True) + jnp.sum(r2_ref[...], axis=1, keepdims=True)
        new_ref[...] = a_ref[...] + jnp.broadcast_to(jnp.log(total) * LOG2E, new_ref.shape)

    span = LANES * unroll

    def chunk(step, carry):
        base = pl.multiple_of(step * span, span)
        accs = [jnp.zeros((8, LANES), F32) for _ in range(unroll)]
        for r in range(0, tokens, GROUP):
            offset = new_ref[r : r + GROUP, :]
            for j in range(unroll):
                x = t_ref[r : r + GROUP, pl.ds(base + j * LANES, LANES)].astype(F32)
                e = jnp.exp2(x * TEACH - offset)
                accs[j] = accs[j] + (e[:8] + e[8:])
        for j in range(unroll):
            out_ref[0, :, pl.ds(base + j * LANES, LANES)] = jnp.sum(
                accs[j], axis=0, keepdims=True
            )
        return carry

    lax.fori_loop(0, block // span, chunk, 0)


def column_pass(teacher, offset, row_here, row_there, shard):
    tokens, width = teacher.shape
    block = shard
    owners = width // shard
    whole = pl.BlockSpec((tokens, LANES), lambda i: (0, 0))
    return pl.pallas_call(
        lambda *refs: column_kernel(*refs, unroll=min(16, shard // LANES)),
        grid=(width // block,),
        in_specs=[pl.BlockSpec(memory_space=pltpu.HBM), whole, whole, whole],
        scratch_shapes=teacher_scratch(teacher, block),
        out_specs=[pl.BlockSpec((1, 1, shard), lambda i: (i, 0, 0)), whole],
        out_shape=[
            jax.ShapeDtypeStruct((owners, 1, shard), F32),
            jax.ShapeDtypeStruct((tokens, LANES), F32),
        ],
        compiler_params=params(),
        name="column_sums",
    )(in_hbm(teacher), offset, row_here, row_there)


def row_kernel(teacher, a_ref, c_ref, out_ref, col_ref, buf, sems, *, unroll, balance):
    t_ref = teacher_block(teacher, buf, sems)
    tokens, block = t_ref.shape
    span = LANES * unroll
    col_ref[...] = balance / c_ref[0]

    @pl.when(pl.program_id(0) == 0)
    def _():
        out_ref[...] = jnp.zeros_like(out_ref)

    def chunk(step, carry):
        base = pl.multiple_of(step * span, span)
        cols = [
            jnp.broadcast_to(col_ref[:, pl.ds(base + j * LANES, LANES)], (GROUP, LANES))
            for j in range(unroll)
        ]
        for r in range(0, tokens, GROUP):
            offset = a_ref[r : r + GROUP, :]
            acc = out_ref[r : r + GROUP, :]
            for j in range(unroll):
                x = t_ref[r : r + GROUP, pl.ds(base + j * LANES, LANES)].astype(F32)
                acc = acc + jnp.exp2(x * TEACH - offset) * cols[j]
            out_ref[r : r + GROUP, :] = acc
        return carry

    lax.fori_loop(0, block // span, chunk, 0)


def row_pass(teacher, offset, sums, balance):
    tokens, width = teacher.shape
    owners, _, block = sums.shape
    whole = pl.BlockSpec((tokens, LANES), lambda i: (0, 0))
    cols = pl.BlockSpec((1, block), lambda i: (0, i))
    return pl.pallas_call(
        lambda *refs: row_kernel(*refs, unroll=min(16, block // LANES), balance=balance),
        grid=(width // block,),
        in_specs=[
            pl.BlockSpec(memory_space=pltpu.HBM),
            whole,
            pl.BlockSpec((1, 1, block), lambda i: (i, 0, 0)),
        ],
        scratch_shapes=teacher_scratch(teacher, block),
        out_specs=[whole, cols],
        out_shape=[
            jax.ShapeDtypeStruct((tokens, LANES), F32),
            jax.ShapeDtypeStruct((1, width), F32),
        ],
        compiler_params=params(),
        name="row_sums",
    )(in_hbm(teacher), offset, sums)


def parts_of_left(hi, lo, axis):
    return jnp.concatenate([hi, lo, hi], axis=axis)


def parts_of_right(hi, lo, axis):
    return jnp.concatenate([hi, hi, lo], axis=axis)


def student_kernel(u_ref, w_ref, m_ref, s_ref, score_a, score_b):
    rows, tokens = score_a.shape
    held = (score_b, score_a)
    step = pl.program_id(0)

    def scores(start):
        w_hi, w_lo = split(w_ref[start : start + rows, :])
        return dot(parts_of_left(w_hi, w_lo, 1), u_ref[...])

    def merge(logits, largest, total):
        logits = logits.reshape(rows // 8, 8, tokens)
        best = jnp.maximum(largest, jnp.max(logits, axis=0))
        fresh = jnp.sum(jnp.exp2(logits - best[None]), axis=0)
        return best, total * jnp.exp2(largest - best) + fresh

    @pl.when(step == 0)
    def _():
        m_ref[...] = jnp.full_like(m_ref, -1e30)
        s_ref[...] = jnp.zeros_like(s_ref)
        score_b[...] = jnp.full_like(score_b, -1e30)

    stats = m_ref[...], s_ref[...]
    pieces = w_ref.shape[0] // rows
    for i in range(pieces):
        held[(i + 1) % 2][...] = scores(i * rows)
        stats = merge(held[i % 2][...], *stats)
    m_ref[...], s_ref[...] = stats

    @pl.when(step == pl.num_programs(0) - 1)
    def _():
        m_ref[...], s_ref[...] = merge(score_b[...], m_ref[...], s_ref[...])


def student_pass(u_turned, protos):
    tokens = u_turned.shape[1]
    rows, depth = protos.shape
    block = min(rows // 2, 2048)
    stat = pl.BlockSpec((8, tokens), lambda i: (0, 0))
    shape = jax.ShapeDtypeStruct((8, tokens), F32)
    return pl.pallas_call(
        student_kernel,
        grid=(rows // block,),
        in_specs=[
            pl.BlockSpec(u_turned.shape, lambda i: (0, 0)),
            pl.BlockSpec((block, depth), lambda i: (i, 0)),
        ],
        out_specs=[stat, stat],
        out_shape=[shape, shape],
        scratch_shapes=[pltpu.VMEM((min(block // 2, 512), tokens), F32)] * 2,
        compiler_params=params(STREAM_LIMIT),
        name="student_stats",
    )(u_turned, in_hbm(protos))


def grad_kernel(own, u_parts, t_parts, lse, offset, tok_in, teacher, *refs, slots, arrivals, parity):
    blocks = len(slots)
    cols, protos = refs[:blocks], refs[blocks : 2 * blocks]
    arrived = refs[2 * blocks : 2 * blocks + arrivals]
    outs = refs[2 * blocks + arrivals : 3 * blocks + arrivals]
    tok_out, teach, sems = refs[3 * blocks + arrivals :]
    width, block = teach.shape[2], protos[0].shape[0]
    step = pl.program_id(0)

    def fetch(i):
        start = pl.multiple_of(own[slots[i]] * width, LANES)
        return pltpu.make_async_copy(teacher.at[:, pl.ds(start, width)], teach.at[i], sems.at[i])

    @pl.when(step == 0)
    def _():
        for i in range(blocks):
            fetch(i).start()
        tok_out[...] = tok_in[...]

    columns = pl.ds(pl.multiple_of(step * block, LANES), block)
    token_part = tok_out[...]
    lse_col = lse[:, :1]
    off_col = offset[:, :1]
    for i in range(blocks):
        w_hi, w_lo = split(protos[i][...])
        logits = dot(u_parts[...], parts_of_right(w_hi, w_lo, 1), ((1,), (1,)))
        student = jnp.exp2(logits - lse_col)

        @pl.when(step == 0)
        def _():
            fetch(i).wait()

        target = jnp.exp2(teach[i, :, columns].astype(F32) * TEACH - off_col) * cols[i][...]
        g_hi, g_lo = split(student - target)
        part = dot(t_parts[...], parts_of_right(g_hi, g_lo, 0))
        if arrivals == 1:
            odd = own[parity].astype(F32)
            part = part + arrived[0][...] * (odd if i == 0 else 1.0 - odd)
        elif arrivals:
            part = part + arrived[i][...]
        outs[i][...] = part
        token_part = token_part + dot(parts_of_left(g_hi, g_lo, 1), parts_of_right(w_hi, w_lo, 0))
    tok_out[...] = token_part


def grad_step(own, slots, consts, tok, teacher, cols, protos, arrived, width):
    tokens, depth = tok.shape
    block = min(width, 512)
    count = width // block
    blocks = len(slots)

    def whole(shape):
        return pl.BlockSpec(shape, lambda g, own: (0, 0))

    def across(shape):
        return pl.BlockSpec(shape, lambda g, own: (0, g))

    def picked(shape, slot):
        return pl.BlockSpec(shape, lambda g, own: (0, own[slot] * count + g))

    def rows(shape, slot):
        return pl.BlockSpec(shape, lambda g, own: (own[slot] * count + g, 0))

    grid = pltpu.PrefetchScalarGridSpec(
        num_scalar_prefetch=1,
        grid=(count,),
        in_specs=[whole(c.shape) for c in consts]
        + [whole(tok.shape)]
        + [pl.BlockSpec(memory_space=pltpu.HBM)]
        + [picked((1, block), slot) for slot in slots]
        + [rows((block, depth), slot) for slot in slots]
        + [across((depth, block)) for x in arrived],
        out_specs=[across((depth, block)) for slot in slots] + [whole(tok.shape)],
        scratch_shapes=[
            pltpu.VMEM((blocks, tokens, width), teacher.dtype),
            pltpu.SemaphoreType.DMA((blocks,)),
        ],
    )
    *parts, tok = pl.pallas_call(
        lambda *refs: grad_kernel(
            *refs, slots=slots, arrivals=len(arrived), parity=own.shape[0] - 1
        ),
        grid_spec=grid,
        out_shape=[jax.ShapeDtypeStruct((depth, width), F32) for slot in slots]
        + [jax.ShapeDtypeStruct(tok.shape, F32)],
        compiler_params=params(),
        name="grad_blocks",
    )(
        own,
        *consts,
        tok,
        in_hbm(teacher),
        *([cols] * blocks),
        *([protos] * blocks),
        *arrived,
    )
    return parts, tok


def proto_kernel(turned, gain, a, b, c, *refs):
    grad_ref, gains_ref = refs[-2:]
    summed = a[...] + (b[...] + c[...])
    protos = turned[...]
    norm = jnp.sqrt(jnp.sum(protos * protos, axis=0, keepdims=True) + EPS)
    unit = protos / norm
    gain_dot = jnp.sum(unit * summed, axis=0, keepdims=True)
    grad = gain[...] / (TEMP_S * norm) * (summed - unit * gain_dot)
    grad_ref[...] = grad.T
    gains_ref[...] = gain_dot / TEMP_S


def proto_grads(turned, gain_row, parts, half, done):
    depth, width = parts[0].shape
    block = min(width, 512)
    count = width // block
    return pl.pallas_call(
        proto_kernel,
        grid=(count,),
        in_specs=[
            pl.BlockSpec((depth, block), lambda i: (0, half * count + i)),
            pl.BlockSpec((1, block), lambda i: (0, half * count + i)),
        ]
        + [pl.BlockSpec((depth, block), lambda i: (0, i))] * 3
        + [pl.BlockSpec(memory_space=pl.ANY)] * len(done),
        out_specs=[
            pl.BlockSpec((block, depth), lambda i: (half * count + i, 0)),
            pl.BlockSpec((1, block), lambda i: (0, half * count + i)),
        ],
        out_shape=[
            jax.ShapeDtypeStruct((2 * width, depth), F32),
            jax.ShapeDtypeStruct((1, 2 * width), F32),
        ],
        input_output_aliases={5 + i: i for i in range(len(done))},
        compiler_params=params(),
        name="proto_grads",
    )(turned, gain_row, *parts, *done)


def token_kernel(here, there, unit, inverse, after, out):
    token_sum = here[...] + there[...]
    inner = jnp.sum(unit[...] * token_sum, axis=1, keepdims=True)
    out[...] = (token_sum - unit[...] * inner) * inverse[...][:, :1]


def token_grads(here, there, unit, inverse, after):
    vmem = pl.BlockSpec(memory_space=pltpu.VMEM)
    return pl.pallas_call(
        token_kernel,
        in_specs=[vmem] * 4 + [pl.BlockSpec(memory_space=pl.ANY)],
        out_specs=vmem,
        out_shape=jax.ShapeDtypeStruct(unit.shape, F32),
        compiler_params=params(),
        name="token_grads",
    )(here, there, unit, inverse, after)


def halves(count):
    return [1 << bit for bit in range(count.bit_length() - 1)]


def swap(x, axis, count, distance):
    return lax.ppermute(x, axis, [(i, i ^ distance) for i in range(count)])


def sum_pair(x, axis, count):
    steps = halves(count)
    for distance in steps[:-1]:
        x = x + swap(x, axis, count, distance)
    return x, swap(x, axis, count, steps[-1])


def column_total(x):
    mine = jnp.sum(lax.all_to_all(x, "dp", 0, 0, tiled=True), axis=0, keepdims=True)
    return lax.all_to_all(jnp.broadcast_to(mine, x.shape), "dp", 0, 0, tiled=True)


def log_total(largest, total, axis, count):
    stats = jnp.stack([largest, total])
    for distance in halves(count):
        other = swap(stats, axis, count, distance)
        top = jnp.maximum(stats[0], other[0])
        both = stats[1] * jnp.exp2(stats[0] - top) + other[1] * jnp.exp2(other[0] - top)
        stats = jnp.stack([top, both])
    return stats[0] + jnp.log2(stats[1])


def sublane_stats(largest, total):
    top = jnp.max(largest, axis=0)
    return top, jnp.sum(total * jnp.exp2(largest - top[None, :]), axis=0)


def ring_order(count):
    depth = count // 4
    up = [z * 4 + core for z in range(depth) for core in range(2)]
    down = [z * 4 + 2 + core for z in reversed(range(depth)) for core in range(2)]
    return up + down


def body(packed, crop_offsets, masked_patch, teacher_logits, prototypes, gain):
    tokens_here = masked_patch.shape[0]
    crops_here = crop_offsets.shape[0]
    per_crop = tokens_here // crops_here
    dp_count = lax.axis_size("dp")
    proto_count = lax.axis_size("proto")
    slice_cols = teacher_logits.shape[1]
    shard = prototypes.shape[0]
    total_tokens = tokens_here * dp_count
    total_protos = slice_cols * proto_count
    loss_scale = total_protos / math.sqrt(total_tokens)
    balance = total_tokens / total_protos
    width = shard // 2
    half = dp_count // 2

    order = ring_order(dp_count)
    place = {d: p for p, d in enumerate(order)}

    def around(step):
        return [(d, order[(place[d] + step) % dp_count]) for d in range(dp_count)]

    ahead, behind = around(1), around(-1)
    slot_of = np.zeros((dp_count, 2 * dp_count + 1), np.int32)
    for d in range(dp_count):
        slot_of[d, 2 * dp_count] = place[d] % 2
        for far in range(dp_count):
            for sub in range(2):
                slot_of[d, 2 * far + sub] = 2 * order[(place[d] + far) % dp_count] + sub
    own = jnp.asarray(slot_of)[lax.axis_index("dp")]

    def slot(far, sub):
        return 2 * (far % dp_count) + sub

    proto_norm = jnp.sqrt(jnp.sum(prototypes * prototypes, axis=1, keepdims=True) + EPS)
    unit_proto = prototypes / proto_norm
    weights = unit_proto * (gain / TEMP_S)[:, None]
    gathered = lax.all_gather(weights, "dp", axis=0, tiled=True)

    crop_of = jnp.arange(tokens_here, dtype=jnp.int32) // per_crop
    match = crop_of[:, None] == jnp.arange(crops_here, dtype=jnp.int32)[None, :]
    starts = jnp.sum(jnp.where(match, crop_offsets[None, :], 0), axis=1)
    row_index = starts + masked_patch
    picked = jnp.take(packed, row_index, axis=0)
    inverse = lax.rsqrt(jnp.sum(picked * picked, axis=1, keepdims=True) + EPS)
    unit_tok = picked * inverse

    def pieces(x):
        hi = lax.reduce_precision(x, 8, 7)
        return hi.astype(BF16), (x - hi).astype(BF16)

    u_hi, u_lo = pieces(unit_tok * LOG2E)
    u_parts = parts_of_left(u_hi, u_lo, 1)
    u_turned = parts_of_right(u_hi, u_lo, 1).T
    t_parts = parts_of_left(*pieces(unit_tok.T), 1)

    top, total = teacher_stats(teacher_logits)
    base = log_total(top[:, 0], jnp.sum(total, axis=1), "proto", proto_count)
    offset = jnp.broadcast_to(base[:, None], (tokens_here, LANES))
    lane = lax.broadcasted_iota(jnp.int32, (tokens_here, LANES), 1)
    row_here = jnp.where(lane == 0, 1.0, 0.0).astype(F32)
    row_there = jnp.zeros((tokens_here, LANES), F32)
    for sweep in range(ITERS):
        sums, offset = column_pass(teacher_logits, offset, row_here, row_there, shard)
        sums = column_total(sums)
        rows, cols = row_pass(teacher_logits, offset, sums, balance)
        row_here, row_there = sum_pair(rows, "proto", proto_count)
    row_sum = jnp.sum(row_here, axis=1) + jnp.sum(row_there, axis=1)
    offset = offset + jnp.log2(row_sum)[:, None]
    cols = cols * loss_scale

    largest, total = student_pass(u_turned, gathered)
    lse = log_total(*sublane_stats(largest, total), "proto", proto_count) - math.log2(loss_scale)
    lse = jnp.broadcast_to(lse[:, None], (tokens_here, LANES))

    token_part = jnp.zeros(unit_tok.shape, F32)
    consts = (u_parts, t_parts, lse, offset)

    def blocks_of(slots, arrived):
        return grad_step(
            own, slots, consts, token_part, teacher_logits, cols, gathered, arrived, width
        )

    crossed = [None, None]
    for sub in range(2):
        (part,), token_part = blocks_of((slot(half, sub),), [])
        crossed[sub] = swap(part, "dp", dp_count, 1)
    waiting = [[crossed[0]], [crossed[1]]]
    mine = []
    for far in range(half - 1, 0, -1):
        if len(mine) < 2 and far <= half // 2 + 1:
            (part,), token_part = blocks_of((slot(0, len(mine)),), [])
            mine.append(part)
        for sub in range(2):
            (first, second), token_part = blocks_of(
                (slot(far, sub), slot(-far, sub)),
                waiting[sub],
            )
            waiting[sub] = [
                lax.ppermute(first, "dp", ahead),
                lax.ppermute(second, "dp", behind),
            ]
    token_here, token_there = sum_pair(token_part, "proto", proto_count)
    turned, gain_row = prototypes.T, gain[None, :]
    grads = proto_grads(turned, gain_row, [mine[0], *waiting[0]], 0, ())
    input_grad = token_grads(
        token_here,
        token_there,
        unit_tok,
        jnp.broadcast_to(inverse, (tokens_here, LANES)),
        grads[1],
    )
    grads = proto_grads(turned, gain_row, [mine[1], *waiting[1]], 1, grads)
    grad_proto, grad_gain = grads[0], grads[1].reshape(shard)
    grad_packed = jnp.zeros(packed.shape, F32).at[row_index].set(input_grad)
    return (grad_packed, grad_proto, grad_gain)


def solution(mesh):
    placed = (
        P("dp", None),
        P("dp"),
        P("dp"),
        P("dp", "proto"),
        P(("proto", "dp"), None),
        P(("proto", "dp")),
    )
    return jax.shard_map(
        body,
        mesh=mesh,
        in_specs=placed,
        out_specs=(P("dp", None), P(("proto", "dp"), None), P(("proto", "dp"))),
        check_vma=False,
    )
```

```python
import math

import jax
import jax.numpy as jnp
import numpy as np
from jax import lax
from jax.experimental import pallas as pl
from jax.experimental.pallas import tpu as pltpu
from jax.sharding import PartitionSpec as P

ITERS = 3
TEMP_S = 0.1
TEMP_T = 0.07
EPS = 1e-06
LOG2E = math.log2(math.e)
TEACH = LOG2E / TEMP_T
LANES = 128
GROUP = 16
VMEM_LIMIT = 20 * 1024 * 1024
STREAM_LIMIT = 52 * 1024 * 1024
F32 = jnp.float32
BF16 = jnp.bfloat16


def params(limit=VMEM_LIMIT):
    return pltpu.CompilerParams(vmem_limit_bytes=limit)


def teacher_block(teacher, buf, sems):
    count, _, block = buf.shape
    step = pl.program_id(0)

    def fetch(i, start):
        return pltpu.make_async_copy(
            teacher.at[:, pl.ds(start, block)], buf.at[i], sems.at[i]
        )

    @pl.when(step == 0)
    def _():
        for i in range(count):
            fetch(i, i * block).start()

    fetch(step, pl.multiple_of(step * block, LANES)).wait()
    return buf.at[step]


def teacher_scratch(teacher, block):
    tokens, width = teacher.shape
    count = width // block
    return [pltpu.VMEM((count, tokens, block), teacher.dtype), pltpu.SemaphoreType.DMA((count,))]


def in_hbm(x):
    return pltpu.with_memory_space_constraint(x, pltpu.HBM)


def split(x):
    hi = x.astype(BF16)
    return hi, (x - hi.astype(F32)).astype(BF16)


def dot(a, b, dims=((1,), (0,))):
    return lax.dot_general(a, b, (dims, ((), ())), preferred_element_type=F32)


def teacher_kernel(t_ref, m_ref, s_ref, *, width, unroll):
    span = LANES * unroll
    for r in range(0, t_ref.shape[0], GROUP):

        def largest(step, best):
            base = pl.multiple_of(step * span, span)
            for j in range(unroll):
                x = t_ref[r : r + GROUP, pl.ds(base + j * LANES, LANES)].astype(F32)
                best = jnp.maximum(best, x)
            return best

        best = lax.fori_loop(0, width // span, largest, jnp.full((GROUP, LANES), -jnp.inf, F32))
        top = jnp.broadcast_to(jnp.max(best, axis=1, keepdims=True), (GROUP, LANES)) * TEACH

        def total(step, acc):
            base = pl.multiple_of(step * span, span)
            for j in range(unroll):
                x = t_ref[r : r + GROUP, pl.ds(base + j * LANES, LANES)].astype(F32)
                acc = acc + jnp.exp2(x * TEACH - top)
            return acc

        acc = lax.fori_loop(0, width // span, total, jnp.zeros((GROUP, LANES), F32))
        m_ref[r : r + GROUP, :] = top
        s_ref[r : r + GROUP, :] = acc


def teacher_stats(teacher):
    tokens, width = teacher.shape
    rows = 32
    shape = jax.ShapeDtypeStruct((tokens, LANES), F32)
    spec = pl.BlockSpec((rows, LANES), lambda i: (i, 0))
    return pl.pallas_call(
        lambda *refs: teacher_kernel(*refs, width=width, unroll=16),
        grid=(tokens // rows,),
        in_specs=[pl.BlockSpec((rows, width), lambda i: (i, 0))],
        out_specs=[spec, spec],
        out_shape=[shape, shape],
        compiler_params=params(STREAM_LIMIT),
        name="teacher_stats",
    )(in_hbm(teacher))


def column_kernel(teacher, a_ref, r1_ref, r2_ref, out_ref, new_ref, buf, sems, *, unroll):
    t_ref = teacher_block(teacher, buf, sems)
    tokens, block = t_ref.shape

    @pl.when(pl.program_id(0) == 0)
    def _():
        total = jnp.sum(r1_ref[...], axis=1, keepdims=True) + jnp.sum(r2_ref[...], axis=1, keepdims=True)
        new_ref[...] = a_ref[...] + jnp.broadcast_to(jnp.log(total) * LOG2E, new_ref.shape)

    span = LANES * unroll

    def chunk(step, carry):
        base = pl.multiple_of(step * span, span)
        accs = [jnp.zeros((8, LANES), F32) for _ in range(unroll)]
        for r in range(0, tokens, GROUP):
            offset = new_ref[r : r + GROUP, :]
            for j in range(unroll):
                x = t_ref[r : r + GROUP, pl.ds(base + j * LANES, LANES)].astype(F32)
                e = jnp.exp2(x * TEACH - offset)
                accs[j] = accs[j] + (e[:8] + e[8:])
        for j in range(unroll):
            out_ref[0, :, pl.ds(base + j * LANES, LANES)] = jnp.sum(
                accs[j], axis=0, keepdims=True
            )
        return carry

    lax.fori_loop(0, block // span, chunk, 0)


def column_pass(teacher, offset, row_here, row_there, shard):
    tokens, width = teacher.shape
    block = shard
    owners = width // shard
    whole = pl.BlockSpec((tokens, LANES), lambda i: (0, 0))
    return pl.pallas_call(
        lambda *refs: column_kernel(*refs, unroll=min(16, shard // LANES)),
        grid=(width // block,),
        in_specs=[pl.BlockSpec(memory_space=pltpu.HBM), whole, whole, whole],
        scratch_shapes=teacher_scratch(teacher, block),
        out_specs=[pl.BlockSpec((1, 1, shard), lambda i: (i, 0, 0)), whole],
        out_shape=[
            jax.ShapeDtypeStruct((owners, 1, shard), F32),
            jax.ShapeDtypeStruct((tokens, LANES), F32),
        ],
        compiler_params=params(),
        name="column_sums",
    )(in_hbm(teacher), offset, row_here, row_there)


def row_kernel(teacher, a_ref, c_ref, out_ref, col_ref, buf, sems, *, unroll, balance):
    t_ref = teacher_block(teacher, buf, sems)
    tokens, block = t_ref.shape
    span = LANES * unroll
    col_ref[...] = balance / c_ref[0]

    @pl.when(pl.program_id(0) == 0)
    def _():
        out_ref[...] = jnp.zeros_like(out_ref)

    def chunk(step, carry):
        base = pl.multiple_of(step * span, span)
        cols = [
            jnp.broadcast_to(col_ref[:, pl.ds(base + j * LANES, LANES)], (GROUP, LANES))
            for j in range(unroll)
        ]
        for r in range(0, tokens, GROUP):
            offset = a_ref[r : r + GROUP, :]
            acc = out_ref[r : r + GROUP, :]
            for j in range(unroll):
                x = t_ref[r : r + GROUP, pl.ds(base + j * LANES, LANES)].astype(F32)
                acc = acc + jnp.exp2(x * TEACH - offset) * cols[j]
            out_ref[r : r + GROUP, :] = acc
        return carry

    lax.fori_loop(0, block // span, chunk, 0)


def row_pass(teacher, offset, sums, balance):
    tokens, width = teacher.shape
    owners, _, block = sums.shape
    whole = pl.BlockSpec((tokens, LANES), lambda i: (0, 0))
    cols = pl.BlockSpec((1, block), lambda i: (0, i))
    return pl.pallas_call(
        lambda *refs: row_kernel(*refs, unroll=min(16, block // LANES), balance=balance),
        grid=(width // block,),
        in_specs=[
            pl.BlockSpec(memory_space=pltpu.HBM),
            whole,
            pl.BlockSpec((1, 1, block), lambda i: (i, 0, 0)),
        ],
        scratch_shapes=teacher_scratch(teacher, block),
        out_specs=[whole, cols],
        out_shape=[
            jax.ShapeDtypeStruct((tokens, LANES), F32),
            jax.ShapeDtypeStruct((1, width), F32),
        ],
        compiler_params=params(),
        name="row_sums",
    )(in_hbm(teacher), offset, sums)


def parts_of_left(hi, lo, axis):
    return jnp.concatenate([hi, lo, hi], axis=axis)


def parts_of_right(hi, lo, axis):
    return jnp.concatenate([hi, hi, lo], axis=axis)


def student_kernel(u_ref, w_hbm, m_ref, s_ref, w_ref, score_a, score_b, sems):
    piece, tokens = score_a.shape
    held = (score_b, score_a)
    count, rows, _ = w_ref.shape

    def fetch(i):
        start = pl.multiple_of(i * rows, rows)
        return pltpu.make_async_copy(w_hbm.at[pl.ds(start, rows), :], w_ref.at[i], sems.at[i])

    def merge(logits, largest, total):
        logits = logits.reshape(piece // 8, 8, tokens)
        best = jnp.maximum(largest, jnp.max(logits, axis=0))
        fresh = jnp.sum(jnp.exp2(logits - best[None]), axis=0)
        return best, total * jnp.exp2(largest - best) + fresh

    for i in range(count):
        fetch(i).start()
    score_b[...] = jnp.full_like(score_b, -1e30)

    def block(i, stats):
        fetch(i).wait()
        for j in range(rows // piece):
            w_hi, w_lo = split(w_ref[i, j * piece : (j + 1) * piece, :])
            held[(j + 1) % 2][...] = dot(parts_of_left(w_hi, w_lo, 1), u_ref[...])
            stats = merge(held[j % 2][...], *stats)
        return stats

    start = (jnp.full(m_ref.shape, -1e30, F32), jnp.zeros(s_ref.shape, F32))
    stats = lax.fori_loop(0, count, block, start)
    m_ref[...], s_ref[...] = merge(score_b[...], *stats)


def student_pass(u_turned, protos):
    tokens = u_turned.shape[1]
    rows, depth = protos.shape
    block = min(rows // 2, 2048)
    count = rows // block
    vmem = pl.BlockSpec(memory_space=pltpu.VMEM)
    shape = jax.ShapeDtypeStruct((8, tokens), F32)
    return pl.pallas_call(
        student_kernel,
        in_specs=[vmem, pl.BlockSpec(memory_space=pltpu.HBM)],
        out_specs=[vmem, vmem],
        out_shape=[shape, shape],
        scratch_shapes=[
            pltpu.VMEM((count, block, depth), F32),
            pltpu.VMEM((512, tokens), F32),
            pltpu.VMEM((512, tokens), F32),
            pltpu.SemaphoreType.DMA((count,)),
        ],
        compiler_params=params(STREAM_LIMIT),
        name="student_stats",
    )(u_turned, in_hbm(protos))


def grad_kernel(own, u_parts, t_parts, lse, offset, tok_in, *refs, blocks, arrivals, parity):
    teach, cols, protos = refs[:blocks], refs[blocks : 2 * blocks], refs[2 * blocks : 3 * blocks]
    arrived = refs[3 * blocks : 3 * blocks + arrivals]
    outs = refs[3 * blocks + arrivals : 4 * blocks + arrivals]
    tok_out = refs[4 * blocks + arrivals]

    @pl.when(pl.program_id(0) == 0)
    def _():
        tok_out[...] = tok_in[...]

    token_part = tok_out[...]
    lse_col = lse[:, :1]
    off_col = offset[:, :1]
    for i in range(blocks):
        w_hi, w_lo = split(protos[i][...])
        logits = dot(u_parts[...], parts_of_right(w_hi, w_lo, 1), ((1,), (1,)))
        student = jnp.exp2(logits - lse_col)
        target = jnp.exp2(teach[i][...].astype(F32) * TEACH - off_col) * cols[i][...]
        g_hi, g_lo = split(student - target)
        part = dot(t_parts[...], parts_of_right(g_hi, g_lo, 0))
        if arrivals == 1:
            odd = own[parity].astype(F32)
            part = part + arrived[0][...] * (odd if i == 0 else 1.0 - odd)
        elif arrivals:
            part = part + arrived[i][...]
        outs[i][...] = part
        token_part = token_part + dot(parts_of_left(g_hi, g_lo, 1), parts_of_right(w_hi, w_lo, 0))
    tok_out[...] = token_part


def grad_step(own, slots, consts, tok, teacher, cols, protos, arrived, width):
    tokens, depth = tok.shape
    block = min(width, 512)
    count = width // block
    blocks = len(slots)

    def whole(shape):
        return pl.BlockSpec(shape, lambda g, own: (0, 0))

    def across(shape):
        return pl.BlockSpec(shape, lambda g, own: (0, g))

    def picked(shape, slot):
        return pl.BlockSpec(shape, lambda g, own: (0, own[slot] * count + g))

    def rows(shape, slot):
        return pl.BlockSpec(shape, lambda g, own: (own[slot] * count + g, 0))

    grid = pltpu.PrefetchScalarGridSpec(
        num_scalar_prefetch=1,
        grid=(count,),
        in_specs=[whole(c.shape) for c in consts]
        + [whole(tok.shape)]
        + [picked((tokens, block), slot) for slot in slots]
        + [picked((1, block), slot) for slot in slots]
        + [rows((block, depth), slot) for slot in slots]
        + [across((depth, block)) for x in arrived],
        out_specs=[across((depth, block)) for slot in slots] + [whole(tok.shape)],
    )
    *parts, tok = pl.pallas_call(
        lambda *refs: grad_kernel(
            *refs, blocks=blocks, arrivals=len(arrived), parity=own.shape[0] - 1
        ),
        grid_spec=grid,
        out_shape=[jax.ShapeDtypeStruct((depth, width), F32) for slot in slots]
        + [jax.ShapeDtypeStruct(tok.shape, F32)],
        compiler_params=params(),
        name="grad_blocks",
    )(
        own,
        *consts,
        tok,
        *([in_hbm(teacher)] * blocks),
        *([cols] * blocks),
        *([protos] * blocks),
        *arrived,
    )
    return parts, tok


def proto_kernel(turned, gain, a, b, c, *refs):
    grad_ref, gains_ref = refs[-2:]
    summed = a[...] + (b[...] + c[...])
    protos = turned[...]
    norm = jnp.sqrt(jnp.sum(protos * protos, axis=0, keepdims=True) + EPS)
    unit = protos / norm
    gain_dot = jnp.sum(unit * summed, axis=0, keepdims=True)
    grad = gain[...] / (TEMP_S * norm) * (summed - unit * gain_dot)
    grad_ref[...] = grad.T
    gains_ref[...] = gain_dot / TEMP_S


def proto_grads(turned, gain_row, parts, half, done):
    depth, width = parts[0].shape
    block = min(width, 512)
    count = width // block
    return pl.pallas_call(
        proto_kernel,
        grid=(count,),
        in_specs=[
            pl.BlockSpec((depth, block), lambda i: (0, half * count + i)),
            pl.BlockSpec((1, block), lambda i: (0, half * count + i)),
        ]
        + [pl.BlockSpec((depth, block), lambda i: (0, i))] * 3
        + [pl.BlockSpec(memory_space=pl.ANY)] * len(done),
        out_specs=[
            pl.BlockSpec((block, depth), lambda i: (half * count + i, 0)),
            pl.BlockSpec((1, block), lambda i: (0, half * count + i)),
        ],
        out_shape=[
            jax.ShapeDtypeStruct((2 * width, depth), F32),
            jax.ShapeDtypeStruct((1, 2 * width), F32),
        ],
        input_output_aliases={5 + i: i for i in range(len(done))},
        compiler_params=params(),
        name="proto_grads",
    )(turned, gain_row, *parts, *done)


def token_kernel(here, there, unit, inverse, after, out):
    token_sum = here[...] + there[...]
    inner = jnp.sum(unit[...] * token_sum, axis=1, keepdims=True)
    out[...] = (token_sum - unit[...] * inner) * inverse[...][:, :1]


def token_grads(here, there, unit, inverse, after):
    vmem = pl.BlockSpec(memory_space=pltpu.VMEM)
    return pl.pallas_call(
        token_kernel,
        in_specs=[vmem] * 4 + [pl.BlockSpec(memory_space=pl.ANY)],
        out_specs=vmem,
        out_shape=jax.ShapeDtypeStruct(unit.shape, F32),
        compiler_params=params(),
        name="token_grads",
    )(here, there, unit, inverse, after)


def halves(count):
    return [1 << bit for bit in range(count.bit_length() - 1)]


def swap(x, axis, count, distance):
    return lax.ppermute(x, axis, [(i, i ^ distance) for i in range(count)])


def sum_pair(x, axis, count):
    steps = halves(count)
    for distance in steps[:-1]:
        x = x + swap(x, axis, count, distance)
    return x, swap(x, axis, count, steps[-1])


def column_total(x):
    mine = jnp.sum(lax.all_to_all(x, "dp", 0, 0, tiled=True), axis=0, keepdims=True)
    return lax.all_to_all(jnp.broadcast_to(mine, x.shape), "dp", 0, 0, tiled=True)


def log_total(largest, total, axis, count):
    stats = jnp.stack([largest, total])
    for distance in halves(count):
        other = swap(stats, axis, count, distance)
        top = jnp.maximum(stats[0], other[0])
        both = stats[1] * jnp.exp2(stats[0] - top) + other[1] * jnp.exp2(other[0] - top)
        stats = jnp.stack([top, both])
    return stats[0] + jnp.log2(stats[1])


def sublane_stats(largest, total):
    top = jnp.max(largest, axis=0)
    return top, jnp.sum(total * jnp.exp2(largest - top[None, :]), axis=0)


def ring_order(count):
    depth = count // 4
    up = [z * 4 + core for z in range(depth) for core in range(2)]
    down = [z * 4 + 2 + core for z in reversed(range(depth)) for core in range(2)]
    return up + down


def body(packed, crop_offsets, masked_patch, teacher_logits, prototypes, gain):
    tokens_here = masked_patch.shape[0]
    crops_here = crop_offsets.shape[0]
    per_crop = tokens_here // crops_here
    dp_count = lax.axis_size("dp")
    proto_count = lax.axis_size("proto")
    slice_cols = teacher_logits.shape[1]
    shard = prototypes.shape[0]
    total_tokens = tokens_here * dp_count
    total_protos = slice_cols * proto_count
    loss_scale = total_protos / math.sqrt(total_tokens)
    balance = total_tokens / total_protos
    width = shard // 2
    half = dp_count // 2

    order = ring_order(dp_count)
    place = {d: p for p, d in enumerate(order)}

    def around(step):
        return [(d, order[(place[d] + step) % dp_count]) for d in range(dp_count)]

    ahead, behind = around(1), around(-1)
    slot_of = np.zeros((dp_count, 2 * dp_count + 1), np.int32)
    for d in range(dp_count):
        slot_of[d, 2 * dp_count] = place[d] % 2
        for far in range(dp_count):
            for sub in range(2):
                slot_of[d, 2 * far + sub] = 2 * order[(place[d] + far) % dp_count] + sub
    own = jnp.asarray(slot_of)[lax.axis_index("dp")]

    def slot(far, sub):
        return 2 * (far % dp_count) + sub

    proto_norm = jnp.sqrt(jnp.sum(prototypes * prototypes, axis=1, keepdims=True) + EPS)
    unit_proto = prototypes / proto_norm
    weights = unit_proto * (gain / TEMP_S)[:, None]
    gathered = lax.all_gather(weights, "dp", axis=0, tiled=True)

    crop_of = jnp.arange(tokens_here, dtype=jnp.int32) // per_crop
    match = crop_of[:, None] == jnp.arange(crops_here, dtype=jnp.int32)[None, :]
    starts = jnp.sum(jnp.where(match, crop_offsets[None, :], 0), axis=1)
    row_index = starts + masked_patch
    picked = jnp.take(packed, row_index, axis=0)
    inverse = lax.rsqrt(jnp.sum(picked * picked, axis=1, keepdims=True) + EPS)
    unit_tok = picked * inverse

    def pieces(x):
        hi = lax.reduce_precision(x, 8, 7)
        return hi.astype(BF16), (x - hi).astype(BF16)

    u_hi, u_lo = pieces(unit_tok * LOG2E)
    u_parts = parts_of_left(u_hi, u_lo, 1)
    u_turned = parts_of_right(u_hi, u_lo, 1).T
    t_parts = parts_of_left(*pieces(unit_tok.T), 1)

    top, total = teacher_stats(teacher_logits)
    base = log_total(top[:, 0], jnp.sum(total, axis=1), "proto", proto_count)
    offset = jnp.broadcast_to(base[:, None], (tokens_here, LANES))
    lane = lax.broadcasted_iota(jnp.int32, (tokens_here, LANES), 1)
    row_here = jnp.where(lane == 0, 1.0, 0.0).astype(F32)
    row_there = jnp.zeros((tokens_here, LANES), F32)
    for sweep in range(ITERS):
        sums, offset = column_pass(teacher_logits, offset, row_here, row_there, shard)
        sums = column_total(sums)
        rows, cols = row_pass(teacher_logits, offset, sums, balance)
        row_here, row_there = sum_pair(rows, "proto", proto_count)
    row_sum = jnp.sum(row_here, axis=1) + jnp.sum(row_there, axis=1)
    offset = offset + jnp.log2(row_sum)[:, None]
    cols = cols * loss_scale

    largest, total = student_pass(u_turned, gathered)
    lse = log_total(*sublane_stats(largest, total), "proto", proto_count) - math.log2(loss_scale)
    lse = jnp.broadcast_to(lse[:, None], (tokens_here, LANES))

    token_part = jnp.zeros(unit_tok.shape, F32)
    consts = (u_parts, t_parts, lse, offset)

    def blocks_of(slots, arrived):
        return grad_step(
            own, slots, consts, token_part, teacher_logits, cols, gathered, arrived, width
        )

    crossed = [None, None]
    for sub in range(2):
        (part,), token_part = blocks_of((slot(half, sub),), [])
        crossed[sub] = swap(part, "dp", dp_count, 1)
    waiting = [[crossed[0]], [crossed[1]]]
    mine = []
    for far in range(half - 1, 0, -1):
        if len(mine) < 2 and far <= half // 2 + 1:
            (part,), token_part = blocks_of((slot(0, len(mine)),), [])
            mine.append(part)
        for sub in range(2):
            (first, second), token_part = blocks_of(
                (slot(far, sub), slot(-far, sub)),
                waiting[sub],
            )
            waiting[sub] = [
                lax.ppermute(first, "dp", ahead),
                lax.ppermute(second, "dp", behind),
            ]
    token_here, token_there = sum_pair(token_part, "proto", proto_count)
    turned, gain_row = prototypes.T, gain[None, :]
    grads = proto_grads(turned, gain_row, [in_hbm(mine[0]), *waiting[0]], 0, ())
    input_grad = token_grads(
        token_here,
        token_there,
        unit_tok,
        jnp.broadcast_to(inverse, (tokens_here, LANES)),
        grads[1],
    )
    grads = proto_grads(turned, gain_row, [in_hbm(mine[1]), *waiting[1]], 1, grads)
    grad_proto, grad_gain = grads[0], grads[1].reshape(shard)
    grad_packed = jnp.zeros(packed.shape, F32).at[row_index].set(input_grad)
    return (grad_packed, grad_proto, grad_gain)


def solution(mesh):
    placed = (
        P("dp", None),
        P("dp"),
        P("dp"),
        P("dp", "proto"),
        P(("proto", "dp"), None),
        P(("proto", "dp")),
    )
    return jax.shard_map(
        body,
        mesh=mesh,
        in_specs=placed,
        out_specs=(P("dp", None), P(("proto", "dp"), None), P(("proto", "dp"))),
        check_vma=False,
    )
```

```python
import math

import jax
import jax.numpy as jnp
import numpy as np
from jax import lax
from jax.experimental import pallas as pl
from jax.experimental.pallas import tpu as pltpu
from jax.sharding import PartitionSpec as P

ITERS = 3
TEMP_S = 0.1
TEMP_T = 0.07
EPS = 1e-06
LOG2E = math.log2(math.e)
TEACH = LOG2E / TEMP_T
LANES = 128
GROUP = 16
VMEM_LIMIT = 20 * 1024 * 1024
STREAM_LIMIT = 52 * 1024 * 1024
F32 = jnp.float32
BF16 = jnp.bfloat16


def params(limit=VMEM_LIMIT):
    return pltpu.CompilerParams(vmem_limit_bytes=limit)


def teacher_block(teacher, buf, sems):
    count, _, block = buf.shape
    step = pl.program_id(0)

    def fetch(i, start):
        return pltpu.make_async_copy(
            teacher.at[:, pl.ds(start, block)], buf.at[i], sems.at[i]
        )

    @pl.when(step == 0)
    def _():
        for i in range(count):
            fetch(i, i * block).start()

    fetch(step, pl.multiple_of(step * block, LANES)).wait()
    return buf.at[step]


def teacher_scratch(teacher, block):
    tokens, width = teacher.shape
    count = width // block
    return [pltpu.VMEM((count, tokens, block), teacher.dtype), pltpu.SemaphoreType.DMA((count,))]


def in_hbm(x):
    return pltpu.with_memory_space_constraint(x, pltpu.HBM)


def split(x):
    hi = x.astype(BF16)
    return hi, (x - hi.astype(F32)).astype(BF16)


def dot(a, b, dims=((1,), (0,))):
    return lax.dot_general(a, b, (dims, ((), ())), preferred_element_type=F32)


def teacher_kernel(t_ref, m_ref, s_ref, *, width, unroll):
    span = LANES * unroll
    for r in range(0, t_ref.shape[0], GROUP):

        def largest(step, best):
            base = pl.multiple_of(step * span, span)
            for j in range(unroll):
                x = t_ref[r : r + GROUP, pl.ds(base + j * LANES, LANES)].astype(F32)
                best = jnp.maximum(best, x)
            return best

        best = lax.fori_loop(0, width // span, largest, jnp.full((GROUP, LANES), -jnp.inf, F32))
        top = jnp.broadcast_to(jnp.max(best, axis=1, keepdims=True), (GROUP, LANES)) * TEACH

        def total(step, acc):
            base = pl.multiple_of(step * span, span)
            for j in range(unroll):
                x = t_ref[r : r + GROUP, pl.ds(base + j * LANES, LANES)].astype(F32)
                acc = acc + jnp.exp2(x * TEACH - top)
            return acc

        acc = lax.fori_loop(0, width // span, total, jnp.zeros((GROUP, LANES), F32))
        m_ref[r : r + GROUP, :] = top
        s_ref[r : r + GROUP, :] = acc


def teacher_stats(teacher):
    tokens, width = teacher.shape
    rows = 32
    shape = jax.ShapeDtypeStruct((tokens, LANES), F32)
    spec = pl.BlockSpec((rows, LANES), lambda i: (i, 0))
    return pl.pallas_call(
        lambda *refs: teacher_kernel(*refs, width=width, unroll=16),
        grid=(tokens // rows,),
        in_specs=[pl.BlockSpec((rows, width), lambda i: (i, 0))],
        out_specs=[spec, spec],
        out_shape=[shape, shape],
        compiler_params=params(STREAM_LIMIT),
        name="teacher_stats",
    )(in_hbm(teacher))


def column_kernel(teacher, a_ref, r1_ref, r2_ref, out_ref, new_ref, buf, sems, *, unroll):
    t_ref = teacher_block(teacher, buf, sems)
    tokens, block = t_ref.shape

    @pl.when(pl.program_id(0) == 0)
    def _():
        total = jnp.sum(r1_ref[...], axis=1, keepdims=True) + jnp.sum(r2_ref[...], axis=1, keepdims=True)
        new_ref[...] = a_ref[...] + jnp.broadcast_to(jnp.log(total) * LOG2E, new_ref.shape)

    span = LANES * unroll

    def chunk(step, carry):
        base = pl.multiple_of(step * span, span)
        accs = [jnp.zeros((8, LANES), F32) for _ in range(unroll)]
        for r in range(0, tokens, GROUP):
            offset = new_ref[r : r + GROUP, :]
            for j in range(unroll):
                x = t_ref[r : r + GROUP, pl.ds(base + j * LANES, LANES)].astype(F32)
                e = jnp.exp2(x * TEACH - offset)
                accs[j] = accs[j] + (e[:8] + e[8:])
        for j in range(unroll):
            out_ref[0, :, pl.ds(base + j * LANES, LANES)] = jnp.sum(
                accs[j], axis=0, keepdims=True
            )
        return carry

    lax.fori_loop(0, block // span, chunk, 0)


def column_pass(teacher, offset, row_here, row_there, shard):
    tokens, width = teacher.shape
    block = shard
    owners = width // shard
    whole = pl.BlockSpec((tokens, LANES), lambda i: (0, 0))
    return pl.pallas_call(
        lambda *refs: column_kernel(*refs, unroll=min(16, shard // LANES)),
        grid=(width // block,),
        in_specs=[pl.BlockSpec(memory_space=pltpu.HBM), whole, whole, whole],
        scratch_shapes=teacher_scratch(teacher, block),
        out_specs=[pl.BlockSpec((1, 1, shard), lambda i: (i, 0, 0)), whole],
        out_shape=[
            jax.ShapeDtypeStruct((owners, 1, shard), F32),
            jax.ShapeDtypeStruct((tokens, LANES), F32),
        ],
        compiler_params=params(),
        name="column_sums",
    )(in_hbm(teacher), offset, row_here, row_there)


def row_kernel(teacher, a_ref, c_ref, out_ref, col_ref, buf, sems, *, unroll, balance):
    t_ref = teacher_block(teacher, buf, sems)
    tokens, block = t_ref.shape
    span = LANES * unroll
    col_ref[...] = balance / c_ref[0]

    @pl.when(pl.program_id(0) == 0)
    def _():
        out_ref[...] = jnp.zeros_like(out_ref)

    def chunk(step, carry):
        base = pl.multiple_of(step * span, span)
        cols = [
            jnp.broadcast_to(col_ref[:, pl.ds(base + j * LANES, LANES)], (GROUP, LANES))
            for j in range(unroll)
        ]
        for r in range(0, tokens, GROUP):
            offset = a_ref[r : r + GROUP, :]
            acc = out_ref[r : r + GROUP, :]
            for j in range(unroll):
                x = t_ref[r : r + GROUP, pl.ds(base + j * LANES, LANES)].astype(F32)
                acc = acc + jnp.exp2(x * TEACH - offset) * cols[j]
            out_ref[r : r + GROUP, :] = acc
        return carry

    lax.fori_loop(0, block // span, chunk, 0)


def row_pass(teacher, offset, sums, balance):
    tokens, width = teacher.shape
    owners, _, block = sums.shape
    whole = pl.BlockSpec((tokens, LANES), lambda i: (0, 0))
    cols = pl.BlockSpec((1, block), lambda i: (0, i))
    return pl.pallas_call(
        lambda *refs: row_kernel(*refs, unroll=min(16, block // LANES), balance=balance),
        grid=(width // block,),
        in_specs=[
            pl.BlockSpec(memory_space=pltpu.HBM),
            whole,
            pl.BlockSpec((1, 1, block), lambda i: (i, 0, 0)),
        ],
        scratch_shapes=teacher_scratch(teacher, block),
        out_specs=[whole, cols],
        out_shape=[
            jax.ShapeDtypeStruct((tokens, LANES), F32),
            jax.ShapeDtypeStruct((1, width), F32),
        ],
        compiler_params=params(),
        name="row_sums",
    )(in_hbm(teacher), offset, sums)


def parts_of_left(hi, lo, axis):
    return jnp.concatenate([hi, lo, hi], axis=axis)


def parts_of_right(hi, lo, axis):
    return jnp.concatenate([hi, hi, lo], axis=axis)


def student_kernel(u_ref, w_hbm, m_ref, s_ref, w_ref, score_a, score_b, sems):
    piece, tokens = score_a.shape
    held = (score_b, score_a)
    count, rows, _ = w_ref.shape

    def fetch(i):
        start = pl.multiple_of(i * rows, rows)
        return pltpu.make_async_copy(w_hbm.at[pl.ds(start, rows), :], w_ref.at[i], sems.at[i])

    def merge(logits, largest, total):
        logits = logits.reshape(piece // 8, 8, tokens)
        best = jnp.maximum(largest, jnp.max(logits, axis=0))
        fresh = jnp.sum(jnp.exp2(logits - best[None]), axis=0)
        return best, total * jnp.exp2(largest - best) + fresh

    for i in range(count):
        fetch(i).start()
    score_b[...] = jnp.full_like(score_b, -1e30)

    def block(i, stats):
        fetch(i).wait()
        for j in range(rows // piece):
            w_hi, w_lo = split(w_ref[i, j * piece : (j + 1) * piece, :])
            held[(j + 1) % 2][...] = dot(parts_of_left(w_hi, w_lo, 1), u_ref[...])
            stats = merge(held[j % 2][...], *stats)
        return stats

    start = (jnp.full(m_ref.shape, -1e30, F32), jnp.zeros(s_ref.shape, F32))
    stats = lax.fori_loop(0, count, block, start)
    m_ref[...], s_ref[...] = merge(score_b[...], *stats)


def student_pass(u_turned, protos):
    tokens = u_turned.shape[1]
    rows, depth = protos.shape
    block = min(rows // 2, 2048)
    count = rows // block
    vmem = pl.BlockSpec(memory_space=pltpu.VMEM)
    shape = jax.ShapeDtypeStruct((8, tokens), F32)
    return pl.pallas_call(
        student_kernel,
        in_specs=[vmem, pl.BlockSpec(memory_space=pltpu.HBM)],
        out_specs=[vmem, vmem],
        out_shape=[shape, shape],
        scratch_shapes=[
            pltpu.VMEM((count, block, depth), F32),
            pltpu.VMEM((256, tokens), F32),
            pltpu.VMEM((256, tokens), F32),
            pltpu.SemaphoreType.DMA((count,)),
        ],
        compiler_params=params(STREAM_LIMIT),
        name="student_stats",
    )(u_turned, in_hbm(protos))


def grad_kernel(own, u_parts, t_parts, lse, offset, tok_in, *refs, blocks, arrivals, parity):
    teach, cols, protos = refs[:blocks], refs[blocks : 2 * blocks], refs[2 * blocks : 3 * blocks]
    arrived = refs[3 * blocks : 3 * blocks + arrivals]
    outs = refs[3 * blocks + arrivals : 4 * blocks + arrivals]
    tok_out = refs[4 * blocks + arrivals]

    @pl.when(pl.program_id(0) == 0)
    def _():
        tok_out[...] = tok_in[...]

    token_part = tok_out[...]
    lse_col = lse[:, :1]
    off_col = offset[:, :1]
    for i in range(blocks):
        w_hi, w_lo = split(protos[i][...])
        logits = dot(u_parts[...], parts_of_right(w_hi, w_lo, 1), ((1,), (1,)))
        student = jnp.exp2(logits - lse_col)
        target = jnp.exp2(teach[i][...].astype(F32) * TEACH - off_col) * cols[i][...]
        g_hi, g_lo = split(student - target)
        part = dot(t_parts[...], parts_of_right(g_hi, g_lo, 0))
        if arrivals == 1:
            odd = own[parity].astype(F32)
            part = part + arrived[0][...] * (odd if i == 0 else 1.0 - odd)
        elif arrivals:
            part = part + arrived[i][...]
        outs[i][...] = part
        token_part = token_part + dot(parts_of_left(g_hi, g_lo, 1), parts_of_right(w_hi, w_lo, 0))
    tok_out[...] = token_part


def grad_step(own, slots, consts, tok, teacher, cols, protos, arrived, width):
    tokens, depth = tok.shape
    block = min(width, 512)
    count = width // block
    blocks = len(slots)

    def whole(shape):
        return pl.BlockSpec(shape, lambda g, own: (0, 0))

    def across(shape):
        return pl.BlockSpec(shape, lambda g, own: (0, g))

    def picked(shape, slot):
        return pl.BlockSpec(shape, lambda g, own: (0, own[slot] * count + g))

    def rows(shape, slot):
        return pl.BlockSpec(shape, lambda g, own: (own[slot] * count + g, 0))

    grid = pltpu.PrefetchScalarGridSpec(
        num_scalar_prefetch=1,
        grid=(count,),
        in_specs=[whole(c.shape) for c in consts]
        + [whole(tok.shape)]
        + [picked((tokens, block), slot) for slot in slots]
        + [picked((1, block), slot) for slot in slots]
        + [rows((block, depth), slot) for slot in slots]
        + [across((depth, block)) for x in arrived],
        out_specs=[across((depth, block)) for slot in slots] + [whole(tok.shape)],
    )
    *parts, tok = pl.pallas_call(
        lambda *refs: grad_kernel(
            *refs, blocks=blocks, arrivals=len(arrived), parity=own.shape[0] - 1
        ),
        grid_spec=grid,
        out_shape=[jax.ShapeDtypeStruct((depth, width), F32) for slot in slots]
        + [jax.ShapeDtypeStruct(tok.shape, F32)],
        compiler_params=params(),
        name="grad_blocks",
    )(
        own,
        *consts,
        tok,
        *([in_hbm(teacher)] * blocks),
        *([cols] * blocks),
        *([protos] * blocks),
        *arrived,
    )
    return parts, tok


def proto_kernel(turned, gain, a, b, c, *refs):
    grad_ref, gains_ref = refs[-2:]
    summed = a[...] + (b[...] + c[...])
    protos = turned[...]
    norm = jnp.sqrt(jnp.sum(protos * protos, axis=0, keepdims=True) + EPS)
    unit = protos / norm
    gain_dot = jnp.sum(unit * summed, axis=0, keepdims=True)
    grad = gain[...] / (TEMP_S * norm) * (summed - unit * gain_dot)
    grad_ref[...] = grad.T
    gains_ref[...] = gain_dot / TEMP_S


def proto_grads(turned, gain_row, parts, half, done):
    depth, width = parts[0].shape
    block = min(width, 512)
    count = width // block
    return pl.pallas_call(
        proto_kernel,
        grid=(count,),
        in_specs=[
            pl.BlockSpec((depth, block), lambda i: (0, half * count + i)),
            pl.BlockSpec((1, block), lambda i: (0, half * count + i)),
        ]
        + [pl.BlockSpec((depth, block), lambda i: (0, i))] * 3
        + [pl.BlockSpec(memory_space=pl.ANY)] * len(done),
        out_specs=[
            pl.BlockSpec((block, depth), lambda i: (half * count + i, 0)),
            pl.BlockSpec((1, block), lambda i: (0, half * count + i)),
        ],
        out_shape=[
            jax.ShapeDtypeStruct((2 * width, depth), F32),
            jax.ShapeDtypeStruct((1, 2 * width), F32),
        ],
        input_output_aliases={5 + i: i for i in range(len(done))},
        compiler_params=params(VMEM_LIMIT // 2),
        name="proto_grads",
    )(turned, gain_row, *parts, *done)


def token_kernel(here, there, unit, inverse, after, out):
    token_sum = here[...] + there[...]
    inner = jnp.sum(unit[...] * token_sum, axis=1, keepdims=True)
    out[...] = (token_sum - unit[...] * inner) * inverse[...][:, :1]


def token_grads(here, there, unit, inverse, after):
    vmem = pl.BlockSpec(memory_space=pltpu.VMEM)
    return pl.pallas_call(
        token_kernel,
        in_specs=[vmem] * 4 + [pl.BlockSpec(memory_space=pl.ANY)],
        out_specs=vmem,
        out_shape=jax.ShapeDtypeStruct(unit.shape, F32),
        compiler_params=params(VMEM_LIMIT // 2),
        name="token_grads",
    )(here, there, unit, inverse, after)


def halves(count):
    return [1 << bit for bit in range(count.bit_length() - 1)]


def swap(x, axis, count, distance):
    return lax.ppermute(x, axis, [(i, i ^ distance) for i in range(count)])


def sum_pair(x, axis, count):
    steps = halves(count)
    for distance in steps[:-1]:
        x = x + swap(x, axis, count, distance)
    return x, swap(x, axis, count, steps[-1])


def column_total(x):
    mine = jnp.sum(lax.all_to_all(x, "dp", 0, 0, tiled=True), axis=0, keepdims=True)
    return lax.all_to_all(jnp.broadcast_to(mine, x.shape), "dp", 0, 0, tiled=True)


def log_total(largest, total, axis, count):
    stats = jnp.stack([largest, total])
    for distance in halves(count):
        other = swap(stats, axis, count, distance)
        top = jnp.maximum(stats[0], other[0])
        both = stats[1] * jnp.exp2(stats[0] - top) + other[1] * jnp.exp2(other[0] - top)
        stats = jnp.stack([top, both])
    return stats[0] + jnp.log2(stats[1])


def sublane_stats(largest, total):
    top = jnp.max(largest, axis=0)
    return top, jnp.sum(total * jnp.exp2(largest - top[None, :]), axis=0)


def ring_order(count):
    depth = count // 4
    up = [z * 4 + core for z in range(depth) for core in range(2)]
    down = [z * 4 + 2 + core for z in reversed(range(depth)) for core in range(2)]
    return up + down


def body(packed, crop_offsets, masked_patch, teacher_logits, prototypes, gain):
    tokens_here = masked_patch.shape[0]
    crops_here = crop_offsets.shape[0]
    per_crop = tokens_here // crops_here
    dp_count = lax.axis_size("dp")
    proto_count = lax.axis_size("proto")
    slice_cols = teacher_logits.shape[1]
    shard = prototypes.shape[0]
    total_tokens = tokens_here * dp_count
    total_protos = slice_cols * proto_count
    loss_scale = total_protos / math.sqrt(total_tokens)
    balance = total_tokens / total_protos
    width = shard // 2
    half = dp_count // 2

    order = ring_order(dp_count)
    place = {d: p for p, d in enumerate(order)}

    def around(step):
        return [(d, order[(place[d] + step) % dp_count]) for d in range(dp_count)]

    ahead, behind = around(1), around(-1)
    slot_of = np.zeros((dp_count, 2 * dp_count + 1), np.int32)
    for d in range(dp_count):
        slot_of[d, 2 * dp_count] = place[d] % 2
        for far in range(dp_count):
            for sub in range(2):
                slot_of[d, 2 * far + sub] = 2 * order[(place[d] + far) % dp_count] + sub
    own = jnp.asarray(slot_of)[lax.axis_index("dp")]

    def slot(far, sub):
        return 2 * (far % dp_count) + sub

    proto_norm = jnp.sqrt(jnp.sum(prototypes * prototypes, axis=1, keepdims=True) + EPS)
    unit_proto = prototypes / proto_norm
    weights = unit_proto * (gain / TEMP_S)[:, None]
    gathered = lax.all_gather(weights, "dp", axis=0, tiled=True)

    crop_of = jnp.arange(tokens_here, dtype=jnp.int32) // per_crop
    match = crop_of[:, None] == jnp.arange(crops_here, dtype=jnp.int32)[None, :]
    starts = jnp.sum(jnp.where(match, crop_offsets[None, :], 0), axis=1)
    row_index = starts + masked_patch
    picked = jnp.take(packed, row_index, axis=0)
    inverse = lax.rsqrt(jnp.sum(picked * picked, axis=1, keepdims=True) + EPS)
    unit_tok = picked * inverse

    def pieces(x):
        hi = lax.reduce_precision(x, 8, 7)
        return hi.astype(BF16), (x - hi).astype(BF16)

    u_hi, u_lo = pieces(unit_tok * LOG2E)
    u_parts = parts_of_left(u_hi, u_lo, 1)
    u_turned = parts_of_right(u_hi, u_lo, 1).T
    t_parts = parts_of_left(*pieces(unit_tok.T), 1)

    top, total = teacher_stats(teacher_logits)
    base = log_total(top[:, 0], jnp.sum(total, axis=1), "proto", proto_count)
    offset = jnp.broadcast_to(base[:, None], (tokens_here, LANES))
    lane = lax.broadcasted_iota(jnp.int32, (tokens_here, LANES), 1)
    row_here = jnp.where(lane == 0, 1.0, 0.0).astype(F32)
    row_there = jnp.zeros((tokens_here, LANES), F32)
    for sweep in range(ITERS):
        sums, offset = column_pass(teacher_logits, offset, row_here, row_there, shard)
        sums = column_total(sums)
        rows, cols = row_pass(teacher_logits, offset, sums, balance)
        row_here, row_there = sum_pair(rows, "proto", proto_count)
    row_sum = jnp.sum(row_here, axis=1) + jnp.sum(row_there, axis=1)
    offset = offset + jnp.log2(row_sum)[:, None]
    cols = cols * loss_scale

    largest, total = student_pass(u_turned, gathered)
    lse = log_total(*sublane_stats(largest, total), "proto", proto_count) - math.log2(loss_scale)
    lse = jnp.broadcast_to(lse[:, None], (tokens_here, LANES))

    token_part = jnp.zeros(unit_tok.shape, F32)
    consts = (u_parts, t_parts, lse, offset)

    def blocks_of(slots, arrived):
        return grad_step(
            own, slots, consts, token_part, teacher_logits, cols, gathered, arrived, width
        )

    crossed = [None, None]
    for sub in range(2):
        (part,), token_part = blocks_of((slot(half, sub),), [])
        crossed[sub] = swap(part, "dp", dp_count, 1)
    waiting = [[crossed[0]], [crossed[1]]]
    mine = []
    for far in range(half - 1, 0, -1):
        if len(mine) < 2 and far <= half // 2 + 1:
            (part,), token_part = blocks_of((slot(0, len(mine)),), [])
            mine.append(part)
        for sub in range(2):
            (first, second), token_part = blocks_of(
                (slot(far, sub), slot(-far, sub)),
                waiting[sub],
            )
            waiting[sub] = [
                lax.ppermute(first, "dp", ahead),
                lax.ppermute(second, "dp", behind),
            ]
    token_here, token_there = sum_pair(token_part, "proto", proto_count)
    turned, gain_row = prototypes.T, gain[None, :]
    grads = proto_grads(turned, gain_row, [in_hbm(mine[0]), *waiting[0]], 0, ())
    input_grad = token_grads(
        token_here,
        token_there,
        unit_tok,
        jnp.broadcast_to(inverse, (tokens_here, LANES)),
        grads[1],
    )
    grads = proto_grads(turned, gain_row, [in_hbm(mine[1]), *waiting[1]], 1, grads)
    grad_proto, grad_gain = grads[0], grads[1].reshape(shard)
    grad_packed = jnp.zeros(packed.shape, F32).at[row_index].set(input_grad)
    return (grad_packed, grad_proto, grad_gain)


def solution(mesh):
    placed = (
        P("dp", None),
        P("dp"),
        P("dp"),
        P("dp", "proto"),
        P(("proto", "dp"), None),
        P(("proto", "dp")),
    )
    return jax.shard_map(
        body,
        mesh=mesh,
        in_specs=placed,
        out_specs=(P("dp", None), P(("proto", "dp"), None), P(("proto", "dp"))),
        check_vma=False,
    )
```
